32 devices in a mesh: groups: 2 (over y), replica: 4 (over x, core), tensor: 4 (over z).
Axes of the slice: x: 2, y: 2, z: 4, core: 2. Of those that a mesh axis runs over, the one named last changes fastest.
Arguments:
- attn_out: bfloat16 [6144, 8192], P(('groups', 'replica'), 'tensor'), parts along dimension 0, may hold values from -6 to 6
- out_weight: bfloat16 [8192, 8192], P('tensor'), may hold values from -0.09375 to 0.09375
- store_factors: bfloat16 [64, 2, 64, 8192], P(('groups', 'replica'), None, None, 'tensor'), parts along dimension 0, may hold values from -1 to 1
- resident_factors: bfloat16 [64, 2, 64, 8192], P(('groups', 'replica'), None, None, 'tensor'), parts along dimension 0, may hold values from -1 to 1
- resident_ids: int32 [8, 8], P(('groups', 'replica')), parts along dimension 0, may hold values from 0 to 31, as said below
- evict_slots: int32 [8, 4], P(('groups', 'replica')), parts along dimension 0, may hold values from 0 to 7, as said below
- incoming: int32 [8, 4], P('groups'), parts along dimension 0, may hold values from 0 to 31, as said below
- store_place: int32 [64], P('groups'), parts along dimension 0, may hold values from 0 to 31, as said below
- req_adapter: int32 [6144], P(('groups', 'replica')), parts along dimension 0, may hold values from 0 to 31, as said below
Outputs:
- projected: bfloat16 [6144, 8192], P(('groups', 'replica'), 'tensor'), parts along dimension 0
The draws below stay inside these ranges and needn't reach their ends.
There are 2 independent parts, one for each index of `groups`. The reference program is written for one: setup_inputs(seed, part) draws one part's arguments, and reference() takes and returns one part's arrays. A program takes and returns all parts, laid end to end along the dimension named above; an argument that names none is the same for every part. Nothing has to cross between parts.
Inputs may be any that keep to these rules, and one draw needn't show every extreme that they name: `store_place`: a permutation; the owner of adapter a is replica store_place[a] // 8. `resident_ids`: each row holds distinct adapters, none of them among that replica's incoming ones. `evict_slots`: each row holds distinct slots. `incoming`: each row holds distinct adapters: exactly 2 of them from each of 2 distinct owners. `req_adapter`: each request's adapter is held by exactly one of its replica's slots after refilling; every slot serves some request.
All inputs are finite; a program needn't handle non-finite values.
Results may differ from the reference program's by a relative error of at most 0.013.
Values may be sent and summed in bfloat16 or wider, within the bound.
No kernel may reach another device: no remote copies, remote signals or barrier semaphores. Data moves between devices by JAX's collectives and lax.ppermute only.
A program may use at most 192 MiB of HBM per device.

```python
import jax
import jax.numpy as jnp
from jax import lax

D = 8192
RANK = 64
REQ_DEV = 768
SLOTS = 8
EV = 4
CAP = 2
STORE_DEV = 8
ADAPTERS = 32
REQS = 3072
N_REPLICA = 4
N_TENSOR = 4


def plan(key):
    subkeys = jax.random.split(key, 8)
    placing = jax.random.permutation(subkeys[0], ADAPTERS).astype(jnp.int32)
    inverse = jnp.zeros((ADAPTERS,), jnp.int32).at[placing].set(jnp.arange(ADAPTERS, dtype=jnp.int32))
    owner_order = jax.vmap(lambda piece_key: jax.random.permutation(piece_key, N_REPLICA))(jax.random.split(subkeys[1], N_REPLICA)).astype(jnp.int32)
    groups_each = EV // CAP
    chosen = owner_order[:, :groups_each]
    within = jax.vmap(lambda piece_key: jax.random.permutation(piece_key, STORE_DEV)[:CAP])(jax.random.split(subkeys[2], N_REPLICA * groups_each)).astype(jnp.int32)
    positions = chosen[:, :, None] * STORE_DEV + within.reshape(N_REPLICA, groups_each, CAP)
    arriving = inverse[positions.reshape(N_REPLICA, EV)]
    shuffle = jax.vmap(lambda piece_key: jax.random.permutation(piece_key, EV))(jax.random.split(subkeys[3], N_REPLICA)).astype(jnp.int32)
    arriving = jnp.take_along_axis(arriving, shuffle, axis=1)
    scores = jax.vmap(lambda piece_key: jax.random.permutation(piece_key, ADAPTERS))(jax.random.split(subkeys[4], N_REPLICA)).astype(jnp.int32)
    taken_now = jnp.any(arriving[:, :, None] == jnp.arange(ADAPTERS, dtype=jnp.int32)[None, None, :], axis=1)
    scores = scores + ADAPTERS * taken_now.astype(jnp.int32)
    resident = jnp.argsort(scores, axis=1, stable=True)[:, :SLOTS].astype(jnp.int32)
    leaving = jax.vmap(lambda piece_key: jax.random.permutation(piece_key, SLOTS)[:EV])(jax.random.split(subkeys[5], N_REPLICA)).astype(jnp.int32)
    final_ids = jax.vmap(lambda held_ids, spots_out, new_ids: held_ids.at[spots_out].set(new_ids))(resident, leaving, arriving)
    first_pick = jax.random.randint(subkeys[6], (N_REPLICA, REQ_DEV), 0, SLOTS)
    second_pick = jax.random.randint(subkeys[7], (N_REPLICA, REQ_DEV), 0, SLOTS)
    slot_pick = jnp.minimum(first_pick, second_pick).astype(jnp.int32)
    slot_pick = slot_pick.at[:, :SLOTS].set(jnp.broadcast_to(jnp.arange(SLOTS, dtype=jnp.int32)[None, :], (N_REPLICA, SLOTS)))
    requested = jnp.take_along_axis(final_ids, slot_pick, axis=1).reshape(N_REPLICA * REQ_DEV)
    return (placing, resident, leaving, arriving, requested)


def factor_scales():
    shrink_scale = jnp.full((1, 1, 1), D ** (-0.5), jnp.float32)
    expand_scale = jnp.full((1, 1, 1), RANK ** (-0.5), jnp.float32)
    return jnp.concatenate([shrink_scale, expand_scale], axis=0)


def draw_store_place(key, part):
    return plan(key)[0]


def draw_resident_ids(key, part):
    return plan(key)[1]


def draw_evict_slots(key, part):
    return plan(key)[2]


def draw_incoming(key, part):
    return plan(key)[3]


def draw_req_adapter(key, part):
    return plan(key)[4]


def draw_store_factors(key, part):
    key = jax.random.fold_in(key, 11)
    shape = (ADAPTERS, 2, RANK, D)
    values = jnp.clip(jax.random.normal(key, shape, jnp.float32), -3.5, 3.5)
    return (values * factor_scales()[None]).astype(jnp.bfloat16)


def draw_resident_factors(key, part):
    key = jax.random.fold_in(key, 23)
    shape = (SLOTS * N_REPLICA, 2, RANK, D)
    values = jnp.clip(jax.random.normal(key, shape, jnp.float32), -3.5, 3.5)
    return (values * factor_scales()[None]).astype(jnp.bfloat16)


def raised(array, stream_key, source, target, parts, factor):
    def block_of(axis_at):
        return (jnp.arange(array.shape[axis_at]) // (array.shape[axis_at] // parts)).reshape((-1,) + (1,) * (array.ndim - 1 - axis_at))

    first = jax.random.permutation(stream_key, parts)[block_of(target)]
    other_side = (block_of(target) + parts // 2) % parts
    return jnp.where((block_of(source) == first) | (block_of(source) == other_side), factor * array, array)


def block_levels(rng, dims, cuts, smallest, top_value):
    loudness = 1.0
    for dim, blocks in cuts:
        steps = jax.random.uniform(jax.random.fold_in(jax.random.fold_in(rng, 6), dim), (blocks,), jnp.float32, smallest / len(cuts), top_value / len(cuts))
        loudness = loudness * jnp.repeat(jnp.exp(steps), dims[dim] // blocks).reshape((-1,) + (1,) * (len(dims) - 1 - dim))
    return loudness


def gaussian(rng, extent, deviation, limit, cuts=(), kind=jnp.bfloat16):
    values = jax.random.normal(rng, extent, jnp.float32) * deviation
    if len(cuts) > 0:
        values = block_levels(rng, extent, cuts, -0.22, 0.18) * values
    return jnp.clip(values, min=-limit, max=limit).astype(kind)


def bell_draw_with(rng, dims, spread, bound, shards, heavy, held_as=jnp.bfloat16):
    result = spread * jax.random.normal(rng, dims, jnp.float32)
    if shards:
        result = result * block_levels(rng, dims, shards, -0.22, 0.18)
    return jnp.clip(raised(result, jax.random.fold_in(rng, 3), *heavy), -bound, bound).astype(held_as)


def setup_inputs(seed: int = 0, part: int = 0) -> dict:
    streams_of = jax.random.split(jax.random.key(seed), 10)
    part_splits = jax.random.split(jax.random.fold_in(streams_of[9], part), 10)
    attn_out = gaussian(part_splits[0], (REQS, D), 1.0, 6.0, ((0, 4), (1, 4)))
    out_weight = bell_draw_with(streams_of[1], (D, D), D ** -0.5, 0.09375, ((0, 4),), (0, 1, 4, 2.0))
    store_factors = draw_store_factors(jax.random.fold_in(jax.random.fold_in(streams_of[9], part), 71), part)
    resident_factors = draw_resident_factors(jax.random.fold_in(jax.random.fold_in(streams_of[9], part), 71), part)
    resident_ids = draw_resident_ids(jax.random.fold_in(jax.random.fold_in(streams_of[9], part), 71), part)
    evict_slots = draw_evict_slots(jax.random.fold_in(jax.random.fold_in(streams_of[9], part), 71), part)
    incoming = draw_incoming(jax.random.fold_in(jax.random.fold_in(streams_of[9], part), 71), part)
    store_place = draw_store_place(jax.random.fold_in(jax.random.fold_in(streams_of[9], part), 71), part)
    req_adapter = draw_req_adapter(jax.random.fold_in(jax.random.fold_in(streams_of[9], part), 71), part)
    return dict(attn_out=attn_out, out_weight=out_weight, store_factors=store_factors, resident_factors=resident_factors, resident_ids=resident_ids, evict_slots=evict_slots, incoming=incoming, store_place=store_place, req_adapter=req_adapter)


def reference(attn_out, out_weight, store_factors, resident_factors, resident_ids, evict_slots, incoming, store_place, req_adapter):
    block_width = D // N_TENSOR

    def head_block(running, block_index):
        features = lax.dynamic_slice_in_dim(attn_out, block_index * block_width, block_width, 1)
        weight_rows = lax.dynamic_slice_in_dim(out_weight, block_index * block_width, block_width, 0)
        term = jnp.dot(features, weight_rows, preferred_element_type=jnp.float32)
        term = lax.optimization_barrier(term.astype(jnp.bfloat16)).astype(jnp.float32)
        return running + term, None

    head_total, _ = lax.scan(head_block, jnp.zeros((REQS, D), jnp.float32), jnp.arange(N_TENSOR, dtype=jnp.int32))
    pieces = []
    for replica_row in range(N_REPLICA):
        leaving = evict_slots[replica_row]
        arriving = incoming[replica_row]
        held_factors = resident_factors[replica_row * SLOTS:(replica_row + 1) * SLOTS]
        held_factors = held_factors.at[leaving].set(store_factors[store_place[arriving]])
        held_ids = resident_ids[replica_row].at[leaving].set(arriving)
        request_rows = attn_out[replica_row * REQ_DEV:(replica_row + 1) * REQ_DEV]
        wanted = req_adapter[replica_row * REQ_DEV:(replica_row + 1) * REQ_DEV]
        shrink_rows = held_factors[:, 0].reshape(SLOTS * RANK, D)
        expand_rows = held_factors[:, 1].reshape(SLOTS * RANK, D)
        shrunk = lax.dot_general(request_rows, shrink_rows, (((1,), (1,)), ((), ())), preferred_element_type=jnp.float32)
        chosen = jnp.repeat(wanted[:, None] == held_ids[None, :], RANK, axis=1)
        masked = jnp.where(chosen, shrunk, jnp.zeros_like(shrunk)).astype(jnp.bfloat16)
        pieces.append(jnp.dot(masked, expand_rows, preferred_element_type=jnp.float32))
    adapted = jnp.concatenate(pieces, axis=0)
    return (head_total + adapted).astype(jnp.bfloat16)
```

```python
import jax
import jax.numpy as jnp
from jax import lax
from jax.sharding import PartitionSpec as P

PARTS = 2


def send_plan(my_store, place, own, replicas):
    store_rows = my_store.shape[0]
    evicted = place.shape[1]
    owners = place // store_rows
    cap = 2
    earlier = jnp.sum(
        (owners[:, :, None] == owners[:, None, :])
        & (jnp.arange(evicted)[None, None, :] < jnp.arange(evicted)[None, :, None]),
        axis=2,
    ).astype(jnp.int32)
    rows = place - owners * store_rows
    return cap, owners, earlier, rows


def refill(store, resident, resident_ids, evict, incoming, store_place, replicas):
    own = lax.axis_index("replica")
    adapters = store_place.shape[0]
    slots = resident.shape[0]
    matches = incoming[:, :, None] == jnp.arange(adapters, dtype=jnp.int32)[None, None, :]
    place = jnp.sum(jnp.where(matches, store_place[None, None, :], 0), axis=2)
    cap, owners, earlier, rows = send_plan(store, place, own, replicas)
    wanted = (owners == own)[:, :, None] & (earlier[:, :, None] == jnp.arange(cap)[None, None, :])
    rows_for = jnp.sum(jnp.where(wanted, rows[:, :, None], 0), axis=1)
    pieces = []
    for shift in range(replicas):
        target = lax.rem(own + shift, replicas)
        picks = lax.dynamic_index_in_dim(rows_for, target, 0, keepdims=False)
        piece = jnp.concatenate(
            [lax.dynamic_slice_in_dim(store, picks[c], 1, 0) for c in range(cap)], axis=0
        )
        if shift:
            piece = lax.ppermute(
                piece, "replica", [(r, (r + shift) % replicas) for r in range(replicas)]
            )
        pieces.append(piece)
    arrived = jnp.concatenate([resident] + pieces, axis=0)
    my_owner = lax.dynamic_index_in_dim(owners, own, 0, keepdims=False)
    my_earlier = lax.dynamic_index_in_dim(earlier, own, 0, keepdims=False)
    my_ids = lax.dynamic_index_in_dim(incoming, own, 0, keepdims=False)
    where_from = slots + lax.rem(own - my_owner + replicas, replicas) * cap + my_earlier
    replaced = evict[None, :] == jnp.arange(slots, dtype=jnp.int32)[:, None]
    is_new = jnp.any(replaced, axis=1)
    source = jnp.where(
        is_new,
        jnp.sum(jnp.where(replaced, where_from[None, :], 0), axis=1),
        jnp.arange(slots, dtype=jnp.int32),
    )
    ids = jnp.where(is_new, jnp.sum(jnp.where(replaced, my_ids[None, :], 0), axis=1), resident_ids)
    held = jnp.concatenate(
        [lax.dynamic_slice_in_dim(arrived, source[s], 1, 0) for s in range(slots)], axis=0
    )
    return held, ids


def make_local(replicas, tensor):
    def local(
        attn_out,
        out_weight,
        store_factors,
        resident_factors,
        resident_ids,
        evict_slots,
        incoming,
        store_place,
        req_adapter,
    ):
        z = lax.axis_index("tensor")
        width = out_weight.shape[1] // tensor
        part = width // PARTS
        slots = resident_factors.shape[0]
        rank = resident_factors.shape[2]

        def term(block, piece):
            start = jnp.clip(block, 0, tensor - 1) * width + piece * part
            columns = lax.dynamic_slice_in_dim(out_weight, start, part, 1)
            return jnp.dot(attn_out, columns, preferred_element_type=jnp.float32)

        came_right = [None] * PARTS
        came_left = [None] * PARTS
        for step in range(tensor - 1):
            for piece in range(PARTS):
                right = term(tensor - 1 - step + z, piece)
                if came_right[piece] is not None:
                    right = right + came_right[piece].astype(jnp.float32)
                came_right[piece] = lax.ppermute(
                    right.astype(jnp.bfloat16), "tensor", [(d, d + 1) for d in range(step + 1)]
                )
                left = term(step - (tensor - 1 - z), piece)
                if came_left[piece] is not None:
                    left = left + came_left[piece].astype(jnp.float32)
                came_left[piece] = lax.ppermute(
                    left.astype(jnp.bfloat16),
                    "tensor",
                    [(tensor - 1 - d, tensor - 2 - d) for d in range(step + 1)],
                )

        held, ids = refill(
            store_factors,
            resident_factors,
            resident_ids[0],
            evict_slots[0],
            incoming,
            store_place,
            replicas,
        )
        uses = req_adapter[:, None] == ids[None, :]
        shrink_rows = held[:, 0].reshape(slots * rank, -1)
        expand_rows = held[:, 1].reshape(slots * rank, -1)
        shrunk = lax.dot_general(
            attn_out, shrink_rows, (((1,), (1,)), ((), ())), preferred_element_type=jnp.float32
        )
        mine = jnp.zeros((attn_out.shape[0], rank), jnp.float32)
        for s in range(slots):
            mine = mine + jnp.where(uses[:, s : s + 1], shrunk[:, s * rank : (s + 1) * rank], 0.0)
        chosen = lax.psum(mine.astype(jnp.bfloat16), "tensor").astype(jnp.bfloat16)
        masked = jnp.concatenate(
            [jnp.where(uses[:, s : s + 1], chosen, jnp.zeros_like(chosen)) for s in range(slots)],
            axis=1,
        )
        own_block = lax.dynamic_slice_in_dim(out_weight, z * width, width, 1)
        own = jnp.dot(attn_out, own_block, preferred_element_type=jnp.float32)
        own = own + jnp.dot(masked, expand_rows, preferred_element_type=jnp.float32)
        total = jnp.concatenate(
            [
                r.astype(jnp.float32) + l.astype(jnp.float32)
                for r, l in zip(came_right, came_left)
            ],
            axis=1,
        )
        return (own + total).astype(jnp.bfloat16)

    return local


def solution(mesh):
    return jax.shard_map(
        make_local(mesh.shape["replica"], mesh.shape["tensor"]),
        mesh=mesh,
        in_specs=(
            P(("groups", "replica"), "tensor"),
            P("tensor", None),
            P(("groups", "replica"), None, None, "tensor"),
            P(("groups", "replica"), None, None, "tensor"),
            P(("groups", "replica"), None),
            P(("groups", "replica"), None),
            P("groups", None),
            P("groups"),
            P(("groups", "replica")),
        ),
        out_specs=P(("groups", "replica"), "tensor"),
        check_vma=False,
    )
```

```python
import functools

import jax
import jax.numpy as jnp
from jax import lax
from jax.experimental import pallas as pl
from jax.experimental.pallas import tpu as pltpu
from jax.sharding import PartitionSpec as P

SHARES = (1, 1)
CAP = 2
VMEM = 28 * 1024 * 1024
SCALE = 4.0


def cost(flops, elements):
    return pl.CostEstimate(
        flops=int(SCALE * flops), bytes_accessed=int(SCALE * 2 * elements), transcendentals=0
    )


def params():
    return pltpu.CompilerParams(vmem_limit_bytes=VMEM)


ORDER = pl.BlockSpec(memory_space=pl.ANY)


def term_kernel(sums, block_ref, a_ref, w_ref, *rest):
    came, out_ref = rest[:sums], rest[-1]
    total = jnp.dot(a_ref[...], w_ref[...], preferred_element_type=jnp.float32)
    for ref in came:
        total = total + ref[...].astype(jnp.float32)
    out_ref[...] = total.astype(out_ref.dtype)


def tile_of(width):
    return min(512, width // sum(SHARES))


def spans(width):
    tile = tile_of(width)
    found, start = [], 0
    for share in SHARES:
        tiles = share * (width // sum(SHARES)) // tile
        found.append((start, tiles))
        start += tiles
    return found


def term(attn, weight, first_tile, tile, tiles, came, after):
    rows, depth = attn.shape
    piece = pl.BlockSpec((rows, tile), lambda j, b: (0, j))
    return pl.pallas_call(
        functools.partial(term_kernel, len(came)),
        grid_spec=pltpu.PrefetchScalarGridSpec(
            num_scalar_prefetch=1,
            grid=(tiles,),
            in_specs=[
                pl.BlockSpec(memory_space=pltpu.VMEM),
                pl.BlockSpec((depth, tile), lambda j, b: (0, b[0] + j)),
            ]
            + [piece] * len(came)
            + [ORDER] * len(after),
            out_specs=piece,
        ),
        out_shape=jax.ShapeDtypeStruct((rows, tiles * tile), jnp.bfloat16),
        compiler_params=params(),
        cost_estimate=cost(2 * rows * depth * tiles * tile, depth * tiles * tile),
    )(first_tile.reshape(1).astype(jnp.int32), attn, weight, *came, *after)


def exchange(size, hop):
    if size & (size - 1) == 0:
        return [(d, d ^ hop) for d in range(size)], lambda d: d ^ hop
    return [(d, (d + hop) % size) for d in range(size)], lambda d: lax.rem(d + hop, size)


def hop_from(size, here, source):
    if size & (size - 1) == 0:
        return here ^ source
    return lax.rem(here - source + size, size)


def pick_kernel(count, row_ref, *refs):
    for n in range(count):
        refs[count + 1 + n][...] = refs[n][...]


def pick(store, rows, after):
    count = rows.shape[0] // CAP
    shape = (1,) + store.shape[1:]

    def from_spec(n):
        return pl.BlockSpec(shape, lambda c, row: (row[n * CAP + c], 0, 0, 0))

    return pl.pallas_call(
        functools.partial(pick_kernel, count),
        grid_spec=pltpu.PrefetchScalarGridSpec(
            num_scalar_prefetch=1,
            grid=(CAP,),
            in_specs=[from_spec(n) for n in range(count)] + [ORDER],
            out_specs=[pl.BlockSpec(shape, lambda c, row: (c, 0, 0, 0))] * count,
        ),
        out_shape=[jax.ShapeDtypeStruct((CAP,) + store.shape[1:], store.dtype)] * count,
        compiler_params=params(),
        cost_estimate=cost(0, 2 * rows.shape[0] * store[0].size),
    )(rows, *[store] * count, after)


def slots_kernel(count, kind_ref, index_ref, id_ref, a_ref, wanted_ref, *rest):
    from_refs = rest[:count]
    mine_ref, expand_ref, factors = rest[-3:]
    s = pl.program_id(0)
    rank = expand_ref.shape[1]
    here = pl.ds(pl.multiple_of(s * rank, rank), rank)

    for n, ref in enumerate(from_refs):

        @pl.when(kind_ref[s] == n)
        def _():
            factors[here, :] = ref[0, 0]
            expand_ref[0] = ref[0, 1]

    @pl.when(s == pl.num_programs(0) - 1)
    def _():
        shrunk = lax.dot_general(
            a_ref[...], factors[...], (((1,), (1,)), ((), ())), preferred_element_type=jnp.float32
        )
        total = jnp.zeros(mine_ref.shape, jnp.float32)
        for n in range(factors.shape[0] // rank):
            total += jnp.where(wanted_ref[...] == id_ref[n], shrunk[:, n * rank : (n + 1) * rank], 0.0)
        mine_ref[...] = total.astype(mine_ref.dtype)


def hold_slots(attn, wanted, ids, kind, index, sources, after):
    rows, depth = attn.shape
    slots = ids.shape[0]
    rank, width = sources[0].shape[2:]

    def from_spec(n):
        return pl.BlockSpec(
            (1, 2, rank, width), lambda s, kind, index, ids: (index[n * slots + s], 0, 0, 0)
        )

    return pl.pallas_call(
        functools.partial(slots_kernel, len(sources)),
        grid_spec=pltpu.PrefetchScalarGridSpec(
            num_scalar_prefetch=3,
            grid=(slots,),
            in_specs=[
                pl.BlockSpec(memory_space=pltpu.VMEM),
                pl.BlockSpec((rows, 1), lambda s, *_: (0, 0)),
            ]
            + [from_spec(n) for n in range(len(sources))]
            + [ORDER],
            out_specs=[
                pl.BlockSpec((rows, rank), lambda s, *_: (0, 0)),
                pl.BlockSpec((1, rank, width), lambda s, *_: (s, 0, 0)),
            ],
            scratch_shapes=[pltpu.VMEM((slots * rank, width), jnp.bfloat16)],
        ),
        out_shape=[
            jax.ShapeDtypeStruct((rows, rank), jnp.bfloat16),
            jax.ShapeDtypeStruct((slots, rank, width), jnp.bfloat16),
        ],
        compiler_params=params(),
        cost_estimate=cost(2 * rows * depth * slots * rank, 3 * slots * rank * width),
    )(kind, index, ids, attn, wanted, *sources, after)


def join_kernel(mine_ref, theirs_ref, after_ref, out_ref):
    out_ref[...] = (
        mine_ref[...].astype(jnp.float32) + theirs_ref[...].astype(jnp.float32)
    ).astype(out_ref.dtype)


def join(mine, theirs, after):
    whole = pl.BlockSpec(mine.shape, lambda: (0, 0))
    return pl.pallas_call(
        join_kernel,
        in_specs=[whole, whole, ORDER],
        out_specs=whole,
        out_shape=jax.ShapeDtypeStruct(mine.shape, mine.dtype),
        compiler_params=params(),
        cost_estimate=cost(0, 3 * mine.size),
    )(mine, theirs, after)


def own_kernel(block_ref, id_ref, a_ref, w_ref, chosen_ref, wanted_ref, expand_ref, after_ref, out_ref, masked):
    @pl.when(pl.program_id(0) == 0)
    def _():
        chosen = chosen_ref[...]
        rank = chosen.shape[1]
        for n in range(masked.shape[1] // rank):
            masked[:, n * rank : (n + 1) * rank] = jnp.where(
                wanted_ref[...] == id_ref[n], chosen, jnp.zeros_like(chosen)
            )

    out_ref[...] = jnp.dot(
        a_ref[...], w_ref[...], preferred_element_type=jnp.float32
    ) + jnp.dot(masked[...], expand_ref[...], preferred_element_type=jnp.float32)


def own_term(attn, weight, block, chosen, wanted, ids, expand, after):
    rows, depth = attn.shape
    ranks, width = expand.shape
    tile = tile_of(width)
    tiles = width // tile
    return pl.pallas_call(
        own_kernel,
        grid_spec=pltpu.PrefetchScalarGridSpec(
            num_scalar_prefetch=2,
            grid=(tiles,),
            in_specs=[
                pl.BlockSpec(memory_space=pltpu.VMEM),
                pl.BlockSpec((depth, tile), lambda j, b, ids: (0, b[0] * tiles + j)),
                pl.BlockSpec(chosen.shape, lambda j, *_: (0, 0)),
                pl.BlockSpec((rows, 1), lambda j, *_: (0, 0)),
                pl.BlockSpec((ranks, tile), lambda j, *_: (0, j)),
                ORDER,
            ],
            out_specs=pl.BlockSpec((rows, tile), lambda j, *_: (0, j)),
            scratch_shapes=[pltpu.VMEM((rows, ranks), jnp.bfloat16)],
        ),
        out_shape=jax.ShapeDtypeStruct((rows, width), jnp.float32),
        compiler_params=params(),
        cost_estimate=cost(2 * rows * width * (depth + ranks), (depth + ranks) * width + 2 * rows * width),
    )(block.reshape(1).astype(jnp.int32), ids, attn, weight, chosen, wanted, expand, after)


def finish_kernel(own_ref, right_ref, left_ref, *rest):
    out_ref = rest[-1]
    out_ref[...] = (
        own_ref[...] + (right_ref[...].astype(jnp.float32) + left_ref[...].astype(jnp.float32))
    ).astype(out_ref.dtype)


def finish(own, right, left, first_tile, so_far):
    rows, width = own.shape
    tile = tile_of(width)
    here = pl.BlockSpec((rows, tile), lambda j: (0, first_tile + j))
    came = pl.BlockSpec((rows, tile), lambda j: (0, j))
    extra = [] if so_far is None else [so_far]
    return pl.pallas_call(
        finish_kernel,
        grid=(right.shape[1] // tile,),
        in_specs=[here, came, came] + [pl.BlockSpec(memory_space=pl.ANY)] * len(extra),
        out_specs=here,
        out_shape=jax.ShapeDtypeStruct((rows, width), jnp.bfloat16),
        input_output_aliases={3: 0} if extra else {},
        compiler_params=params(),
        cost_estimate=cost(0, 5 * rows * right.shape[1]),
    )(own, right, left, *extra)


def make_local(replicas, tensor):
    def local(
        attn_out,
        out_weight,
        store_factors,
        resident_factors,
        resident_ids,
        evict_slots,
        incoming,
        store_place,
        req_adapter,
    ):
        z = lax.axis_index("tensor")
        own = lax.axis_index("replica")
        width = out_weight.shape[1] // tensor
        tile = tile_of(width)
        pieces = spans(width)
        slots = resident_factors.shape[0]
        store_rows = store_factors.shape[0]
        evict = evict_slots[0]
        to_right = [(d, d + 1) for d in range(tensor - 1)]
        to_left = [(d + 1, d) for d in range(tensor - 1)]

        def product(block, piece, came, after):
            start, tiles = pieces[piece]
            first = jnp.clip(block, 0, tensor - 1) * (width // tile) + start
            return term(attn_out, out_weight, first, tile, tiles, came, [] if after is attn_out else [after])

        def step_of(step, came_right, came_left, after, between):
            right_pairs = to_right[: step + 1]
            left_pairs = to_left[tensor - 2 - step :]
            right_block = tensor - 1 - step + z
            left_block = z + step + 1 - tensor
            rights, lefts = [], []
            for piece in range(len(pieces)):
                right_in = [] if came_right is None else [came_right[piece]]
                left_in = [] if came_left is None else [came_left[piece]]
                if 2 * step < tensor - 1:
                    block = jnp.where(2 * z < tensor, right_block, left_block)
                    same = right_in and right_in[0] is left_in[0]
                    out = product(block, piece, right_in + ([] if same else left_in), after)
                    after = out
                    if 2 * step + 3 < tensor:
                        moved = lax.ppermute(out, "tensor", right_pairs + left_pairs)
                        rights.append(moved)
                        lefts.append(moved)
                    else:
                        rights.append(lax.ppermute(out, "tensor", right_pairs))
                        lefts.append(lax.ppermute(out, "tensor", left_pairs))
                else:
                    out = product(right_block, piece, right_in, after)
                    rights.append(lax.ppermute(out, "tensor", right_pairs))
                    after = out
                    out = product(left_block, piece, left_in, after)
                    lefts.append(lax.ppermute(out, "tensor", left_pairs))
                    after = out
                if piece < len(pieces) - 1 or step == 0:
                    after = between(after)
            return rights, lefts, after

        matches = incoming[:, :, None] == jnp.arange(store_place.shape[0], dtype=jnp.int32)
        place = jnp.sum(jnp.where(matches, store_place, 0), axis=2)
        owners = place // store_rows
        spots = jnp.arange(place.shape[1], dtype=jnp.int32)
        earlier = jnp.sum(
            (owners[:, :, None] == owners[:, None, :]) & (spots[None, :] < spots[:, None]), axis=2
        ).astype(jnp.int32)
        asked = (owners == own)[:, :, None] & (
            earlier[:, :, None] == jnp.arange(CAP, dtype=jnp.int32)
        )
        rows_for = jnp.sum(jnp.where(asked, (place % store_rows)[:, :, None], 0), axis=1)
        hops = [exchange(replicas, hop) for hop in range(1, replicas)]
        send_rows = [
            lax.dynamic_index_in_dim(rows_for, to(own), 0, keepdims=False) for _, to in hops
        ]

        my_place = lax.dynamic_index_in_dim(place, own, 0, keepdims=False)
        my_earlier = lax.dynamic_index_in_dim(earlier, own, 0, keepdims=False)
        my_ids = lax.dynamic_index_in_dim(incoming, own, 0, keepdims=False)
        my_hop = hop_from(replicas, own, my_place // store_rows)
        my_index = jnp.where(my_hop == 0, my_place % store_rows, my_earlier)
        replaced = evict[None, :] == jnp.arange(slots, dtype=jnp.int32)[:, None]
        is_new = jnp.any(replaced, axis=1)

        def per_slot(new, old):
            chosen = jnp.sum(jnp.where(replaced, new[None, :], 0), axis=1)
            return jnp.where(is_new, chosen, old).astype(jnp.int32)

        kind = per_slot(1 + my_hop, jnp.zeros((slots,), jnp.int32))
        place_in = per_slot(my_index, jnp.arange(slots, dtype=jnp.int32))
        ids = per_slot(my_ids, resident_ids[0])
        index = jnp.concatenate(
            [jnp.where(kind == n, place_in, 0) for n in range(1 + replicas)]
        ).astype(jnp.int32)
        wanted = req_adapter[:, None]
        sources = [resident_factors, store_factors]
        state = {"mine": None, "bit": 1, "theirs": None}

        def fetch(after):
            if not send_rows:
                return after
            picked = pick(store_factors, jnp.concatenate(send_rows).astype(jnp.int32), after)
            for piece, (pairs, _) in reversed(list(zip(picked, hops))):
                sources.insert(2, lax.ppermute(piece, "replica", pairs))
            return picked[0]

        def send_mine():
            if state["bit"] < tensor:
                pairs, _ = exchange(tensor, state["bit"])
                state["theirs"] = lax.ppermute(state["mine"], "tensor", pairs)

        def shrink(after):
            state["mine"], state["expand"] = hold_slots(
                attn_out, wanted, ids, kind, index, sources, after
            )
            if tensor & (tensor - 1) == 0:
                send_mine()
            else:
                state["mine"] = lax.psum(state["mine"], "tensor")
            return state["mine"]

        def add_theirs(after):
            if state["theirs"] is None:
                return after
            state["mine"] = join(state["mine"], state["theirs"], after)
            state["bit"] *= 2
            state["theirs"] = None
            send_mine()
            return state["mine"]

        def after_pieces(step):
            if step == 0:
                calls = [None] * (len(pieces) - 1) + [fetch]
            elif step == 1:
                calls = [shrink] + [None] * len(pieces)
            else:
                calls = [None] * len(pieces)
            todo = iter(calls)

            def between(after):
                call = next(todo)
                return after if call is None else call(after)

            return between

        rights, lefts, last = None, None, attn_out
        for step in range(tensor - 1):
            if step > 1:
                last = add_theirs(last)
            rights, lefts, last = step_of(step, rights, lefts, last, after_pieces(step))
        if tensor < 3:
            last = shrink(fetch(last) if tensor == 1 else last)
        while state["theirs"] is not None:
            last = add_theirs(last)
        total = own_term(
            attn_out,
            out_weight,
            z,
            state["mine"],
            wanted,
            ids,
            state["expand"].reshape(-1, width),
            last,
        )
        if tensor == 1:
            return total.astype(jnp.bfloat16)
        out = None
        for piece, (start, _) in enumerate(pieces):
            out = finish(total, rights[piece], lefts[piece], start, out)
        return out

    return local


def solution(mesh):
    return jax.shard_map(
        make_local(mesh.shape["replica"], mesh.shape["tensor"]),
        mesh=mesh,
        in_specs=(
            P(("groups", "replica"), "tensor"),
            P("tensor", None),
            P(("groups", "replica"), None, None, "tensor"),
            P(("groups", "replica"), None, None, "tensor"),
            P(("groups", "replica"), None),
            P(("groups", "replica"), None),
            P("groups", None),
            P("groups"),
            P(("groups", "replica")),
        ),
        out_specs=P(("groups", "replica"), "tensor"),
        check_vma=False,
    )
```

```python
import functools

import jax
import jax.numpy as jnp
from jax import lax
from jax.experimental import pallas as pl
from jax.experimental.pallas import tpu as pltpu
from jax.sharding import PartitionSpec as P

CAP = 2
FIRST = 1
VMEM = 28 * 1024 * 1024
FIRST_VMEM = 60 * 1024 * 1024
SCALE = 3.0


def cost(flops, elements):
    return pl.CostEstimate(
        flops=int(SCALE * flops), bytes_accessed=int(SCALE * 2 * elements), transcendentals=0
    )


def params(vmem=VMEM):
    return pltpu.CompilerParams(vmem_limit_bytes=vmem)


ORDER = pl.BlockSpec(memory_space=pl.ANY)


def term_kernel(ranges, place_ref, a_ref, w_ref, *rest):
    out_ref = rest[-1]
    j = pl.program_id(0)
    total = jnp.dot(a_ref[...], w_ref[...], preferred_element_type=jnp.float32)
    for n, (low, count) in enumerate(ranges):
        counts = (place_ref[1 + n] > 0) & (j >= low) & (j < low + count)
        total += jnp.where(counts, rest[n][...].astype(jnp.float32), 0.0)
    out_ref[...] = total.astype(out_ref.dtype)


def tile_of(width):
    return max(128, width // 8)


def spans(width, first):
    tiles = width // tile_of(width)
    half = tiles // 2
    shares = [half, tiles - half] if half else [tiles]
    if first and half > 2:
        shares = [FIRST, half - FIRST, tiles - half]
    return [(sum(shares[:n]), share) for n, share in enumerate(shares)]


def term(attn, weight, first_tile, tile, tiles, came, after):
    rows, depth = attn.shape
    ranges = [(low, ref.shape[1] // tile) for ref, _, low in came]

    def part_spec(low, count):
        return pl.BlockSpec((rows, tile), lambda j, b: (0, jnp.clip(j - low, 0, count - 1)))

    return pl.pallas_call(
        functools.partial(term_kernel, ranges),
        grid_spec=pltpu.PrefetchScalarGridSpec(
            num_scalar_prefetch=1,
            grid=(tiles,),
            in_specs=[
                pl.BlockSpec(memory_space=pltpu.VMEM),
                pl.BlockSpec((depth, tile), lambda j, b: (0, b[0] + j)),
            ]
            + [part_spec(*span) for span in ranges]
            + [ORDER],
            out_specs=pl.BlockSpec((rows, tile), lambda j, b: (0, j)),
        ),
        out_shape=jax.ShapeDtypeStruct((rows, tiles * tile), jnp.bfloat16),
        compiler_params=params(),
        cost_estimate=cost(2 * rows * depth * tiles * tile, depth * tiles * tile),
    )(
        jnp.stack([first_tile, *[flag for _, flag, _ in came]]).astype(jnp.int32),
        attn,
        weight,
        *[ref for ref, _, _ in came],
        after,
    )


def first_kernel(tile, tiles, place_ref, a_hbm, w_hbm, out_ref, a, w, sems):
    parts, _, step = a.shape
    column = pl.multiple_of(place_ref[0] * tile, tile)
    copies = []
    for k in range(parts):
        copies.append(
            (
                pltpu.make_async_copy(a_hbm.at[:, pl.ds(k * step, step)], a.at[k], sems.at[0, k]),
                pltpu.make_async_copy(
                    w_hbm.at[pl.ds(k * step, step), pl.ds(column, tiles * tile)],
                    w.at[k],
                    sems.at[1, k],
                ),
            )
        )
    for of_a, of_w in copies:
        of_w.start()
        of_a.start()
    total = None
    for k, (of_a, of_w) in enumerate(copies):
        of_w.wait()
        of_a.wait()
        share = jnp.dot(a[k], w[k], preferred_element_type=jnp.float32)
        total = share if total is None else total + share
    out_ref[...] = total.astype(out_ref.dtype)


def first_term(attn, weight, first_tile, tile, tiles):
    rows, depth = attn.shape
    step = min(depth, 512)
    parts = depth // step
    return pl.pallas_call(
        functools.partial(first_kernel, tile, tiles),
        in_specs=[
            pl.BlockSpec(memory_space=pltpu.SMEM),
            pl.BlockSpec(memory_space=pltpu.HBM),
            pl.BlockSpec(memory_space=pltpu.HBM),
        ],
        out_specs=pl.BlockSpec(memory_space=pltpu.VMEM),
        out_shape=jax.ShapeDtypeStruct((rows, tiles * tile), jnp.bfloat16),
        scratch_shapes=[
            pltpu.VMEM((parts, rows, step), attn.dtype),
            pltpu.VMEM((parts, step, tiles * tile), weight.dtype),
            pltpu.SemaphoreType.DMA((2, parts)),
        ],
        compiler_params=params(FIRST_VMEM),
        cost_estimate=cost(2 * rows * depth * tiles * tile, depth * tiles * tile),
    )(first_tile.reshape(1).astype(jnp.int32), attn, weight)


def exchange(size, hop):
    if size & (size - 1) == 0:
        return [(d, d ^ hop) for d in range(size)], lambda d: d ^ hop
    return [(d, (d + hop) % size) for d in range(size)], lambda d: lax.rem(d + hop, size)


def hop_from(size, here, source):
    if size & (size - 1) == 0:
        return here ^ source
    return lax.rem(here - source + size, size)


def pick_kernel(count, row_ref, *refs):
    for n in range(count):
        refs[count + 1 + n][...] = refs[n][...]


def pick(store, rows, after):
    count = rows.shape[0] // CAP
    shape = (1,) + store.shape[1:]

    def from_spec(n):
        return pl.BlockSpec(shape, lambda c, row: (row[n * CAP + c], 0, 0, 0))

    return pl.pallas_call(
        functools.partial(pick_kernel, count),
        grid_spec=pltpu.PrefetchScalarGridSpec(
            num_scalar_prefetch=1,
            grid=(CAP,),
            in_specs=[from_spec(n) for n in range(count)] + [ORDER],
            out_specs=[pl.BlockSpec(shape, lambda c, row: (c, 0, 0, 0))] * count,
        ),
        out_shape=[jax.ShapeDtypeStruct((CAP,) + store.shape[1:], store.dtype)] * count,
        compiler_params=params(),
        cost_estimate=cost(0, 2 * rows.shape[0] * store[0].size),
    )(rows, *[store] * count, after)


def slots_kernel(count, kind_ref, index_ref, id_ref, a_ref, wanted_ref, *rest):
    from_refs = rest[:count]
    mine_ref, expand_ref, factors = rest[-3:]
    s = pl.program_id(0)
    rank = expand_ref.shape[1]
    here = pl.ds(pl.multiple_of(s * rank, rank), rank)

    for n, ref in enumerate(from_refs):

        @pl.when(kind_ref[s] == n)
        def _():
            factors[here, :] = ref[0, 0]
            expand_ref[0] = ref[0, 1]

    @pl.when(s == pl.num_programs(0) - 1)
    def _():
        shrunk = lax.dot_general(
            a_ref[...], factors[...], (((1,), (1,)), ((), ())), preferred_element_type=jnp.float32
        )
        total = jnp.zeros(mine_ref.shape, jnp.float32)
        for n in range(factors.shape[0] // rank):
            total += jnp.where(wanted_ref[...] == id_ref[n], shrunk[:, n * rank : (n + 1) * rank], 0.0)
        mine_ref[...] = total.astype(mine_ref.dtype)


def hold_slots(attn, wanted, ids, kind, index, sources, after):
    rows, depth = attn.shape
    slots = ids.shape[0]
    rank, width = sources[0].shape[2:]

    def from_spec(n):
        return pl.BlockSpec(
            (1, 2, rank, width), lambda s, kind, index, ids: (index[n * slots + s], 0, 0, 0)
        )

    return pl.pallas_call(
        functools.partial(slots_kernel, len(sources)),
        grid_spec=pltpu.PrefetchScalarGridSpec(
            num_scalar_prefetch=3,
            grid=(slots,),
            in_specs=[
                pl.BlockSpec(memory_space=pltpu.VMEM),
                pl.BlockSpec((rows, 1), lambda s, *_: (0, 0)),
            ]
            + [from_spec(n) for n in range(len(sources))]
            + [ORDER],
            out_specs=[
                pl.BlockSpec((rows, rank), lambda s, *_: (0, 0)),
                pl.BlockSpec((1, rank, width), lambda s, *_: (s, 0, 0)),
            ],
            scratch_shapes=[pltpu.VMEM((slots * rank, width), jnp.bfloat16)],
        ),
        out_shape=[
            jax.ShapeDtypeStruct((rows, rank), jnp.bfloat16),
            jax.ShapeDtypeStruct((slots, rank, width), jnp.bfloat16),
        ],
        compiler_params=params(),
        cost_estimate=cost(2 * rows * depth * slots * rank, 3 * slots * rank * width),
    )(kind, index, ids, attn, wanted, *sources, after)


def join_kernel(keep_ref, mine_ref, theirs_ref, after_ref, out_ref):
    out_ref[...] = (
        jnp.where(keep_ref[0] > 0, mine_ref[...].astype(jnp.float32), 0.0)
        + theirs_ref[...].astype(jnp.float32)
    ).astype(out_ref.dtype)


def join(keep, mine, theirs, after):
    whole = pl.BlockSpec(mine.shape, lambda: (0, 0))
    return pl.pallas_call(
        join_kernel,
        in_specs=[pl.BlockSpec(memory_space=pltpu.SMEM), whole, whole, ORDER],
        out_specs=whole,
        out_shape=jax.ShapeDtypeStruct(mine.shape, mine.dtype),
        compiler_params=params(),
        cost_estimate=cost(0, 3 * mine.size),
    )(jnp.reshape(keep, (1,)).astype(jnp.int32), mine, theirs, after)


def own_kernel(block_ref, id_ref, a_ref, w_ref, chosen_ref, wanted_ref, expand_ref, after_ref, out_ref, masked):
    @pl.when(pl.program_id(0) == 0)
    def _():
        chosen = chosen_ref[...]
        rank = chosen.shape[1]
        for n in range(masked.shape[1] // rank):
            masked[:, n * rank : (n + 1) * rank] = jnp.where(
                wanted_ref[...] == id_ref[n], chosen, jnp.zeros_like(chosen)
            )

    out_ref[...] = jnp.dot(
        a_ref[...], w_ref[...], preferred_element_type=jnp.float32
    ) + jnp.dot(masked[...], expand_ref[...], preferred_element_type=jnp.float32)


def own_term(attn, weight, block, chosen, wanted, ids, expand, after):
    rows, depth = attn.shape
    ranks, width = expand.shape
    tile = width // 4
    tiles = 4
    return pl.pallas_call(
        own_kernel,
        grid_spec=pltpu.PrefetchScalarGridSpec(
            num_scalar_prefetch=2,
            grid=(tiles,),
            in_specs=[
                pl.BlockSpec(memory_space=pltpu.VMEM),
                pl.BlockSpec((depth, tile), lambda j, b, ids: (0, b[0] * tiles + j)),
                pl.BlockSpec(chosen.shape, lambda j, *_: (0, 0)),
                pl.BlockSpec((rows, 1), lambda j, *_: (0, 0)),
                pl.BlockSpec((ranks, tile), lambda j, *_: (0, j)),
                ORDER,
            ],
            out_specs=pl.BlockSpec((rows, tile), lambda j, *_: (0, j)),
            scratch_shapes=[pltpu.VMEM((rows, ranks), jnp.bfloat16)],
        ),
        out_shape=jax.ShapeDtypeStruct((rows, width), jnp.float32),
        compiler_params=params(),
        cost_estimate=cost(2 * rows * width * (depth + ranks), (depth + ranks) * width + 2 * rows * width),
    )(block.reshape(1).astype(jnp.int32), ids, attn, weight, chosen, wanted, expand, after)


def finish_kernel(sums, own_ref, *rest):
    out_ref = rest[-1]
    total = own_ref[...]
    for ref in rest[:sums]:
        total += ref[...].astype(jnp.float32)
    out_ref[...] = total.astype(out_ref.dtype)


def finish(own, sums, first_column, so_far):
    rows, width = own.shape
    tile = tile_of(width) * 2
    here = pl.BlockSpec((rows, tile), lambda j: (0, first_column // tile + j))
    came = pl.BlockSpec((rows, tile), lambda j: (0, j))
    extra = [] if so_far is None else [so_far]
    return pl.pallas_call(
        functools.partial(finish_kernel, len(sums)),
        grid=(sums[0].shape[1] // tile,),
        in_specs=[here] + [came] * len(sums) + [pl.BlockSpec(memory_space=pl.ANY)] * len(extra),
        out_specs=here,
        out_shape=jax.ShapeDtypeStruct((rows, width), jnp.bfloat16),
        input_output_aliases={1 + len(sums): 0} if extra else {},
        compiler_params=params(),
        cost_estimate=cost(0, 5 * rows * sums[0].shape[1]),
    )(own, *sums, *extra)


def make_local(replicas, tensor):
    def local(
        attn_out,
        out_weight,
        store_factors,
        resident_factors,
        resident_ids,
        evict_slots,
        incoming,
        store_place,
        req_adapter,
    ):
        z = lax.axis_index("tensor")
        own = lax.axis_index("replica")
        width = out_weight.shape[1] // tensor
        tile = tile_of(width)
        slots = resident_factors.shape[0]
        store_rows = store_factors.shape[0]
        evict = evict_slots[0]
        even, odd = z % 2 == 0, z % 2 == 1
        not_first, not_last = z > 0, z < tensor - 1

        def edges(step, first):
            pairs = []
            for d in range(first, tensor - 1, 2):
                pairs += [(d, d + 1)] * (d <= step)
                pairs += [(d + 1, d)] * (d + 1 >= tensor - 1 - step)
            return pairs

        def swap(pairs):
            return pairs + [(b, a) for a, b in pairs if (b, a) not in pairs]

        def product(block, span, came_a, flag_a, came_b, flag_b, after):
            start, tiles = span
            first = jnp.clip(block, 0, tensor - 1) * (width // tile) + start
            if after is None:
                return first_term(attn_out, out_weight, first, tile, tiles)
            came = []
            for sums, flag in ((came_a, flag_a), (came_b, flag_b)):
                for (low, count), ref in sums:
                    if low < start + tiles and start < low + count:
                        came.append((ref, flag, low - start))
            return term(attn_out, out_weight, first, tile, tiles, came, after)

        def step_of(step, came_x, came_y, after, between):
            right_block = tensor - 1 - step + z
            left_block = z + step + 1 - tensor
            pairs_x, pairs_y = edges(step, 0), edges(step, 1)
            xs, ys = [], []
            for span in spans(width, step == 0):
                if 2 * step < tensor - 1:
                    goes_right = 2 * z < tensor
                    block = jnp.where(goes_right, right_block, left_block)
                    flag_x = jnp.where(goes_right, odd, even & not_last)
                    flag_y = jnp.where(goes_right, even & not_first, odd & not_last)
                    for_x = for_y = product(block, span, came_x, flag_x, came_y, flag_y, after)
                else:
                    flag = jnp.where(even, not_first, not_last)
                    block = jnp.where(even, right_block, left_block)
                    for_x = product(block, span, [], flag, came_y, flag, after)
                    block = jnp.where(even, left_block, right_block)
                    for_y = product(block, span, came_x, flag, [], flag, for_x)
                pairs = pairs_x if step or xs else swap(pairs_x)
                xs.append((span, lax.ppermute(for_x, "tensor", pairs)))
                if pairs_y:
                    ys.append((span, lax.ppermute(for_y, "tensor", pairs_y)))
                after = between(step, len(xs) - 1, for_y)
            return xs, ys, after

        matches = incoming[:, :, None] == jnp.arange(store_place.shape[0], dtype=jnp.int32)
        place = jnp.sum(jnp.where(matches, store_place, 0), axis=2)
        owners = place // store_rows
        spots = jnp.arange(place.shape[1], dtype=jnp.int32)
        earlier = jnp.sum(
            (owners[:, :, None] == owners[:, None, :]) & (spots[None, :] < spots[:, None]), axis=2
        ).astype(jnp.int32)
        asked = (owners == own)[:, :, None] & (
            earlier[:, :, None] == jnp.arange(CAP, dtype=jnp.int32)
        )
        rows_for = jnp.sum(jnp.where(asked, (place % store_rows)[:, :, None], 0), axis=1)
        hops = [exchange(replicas, hop) for hop in range(1, replicas)]
        send_rows = [
            lax.dynamic_index_in_dim(rows_for, to(own), 0, keepdims=False) for _, to in hops
        ]

        my_place = lax.dynamic_index_in_dim(place, own, 0, keepdims=False)
        my_earlier = lax.dynamic_index_in_dim(earlier, own, 0, keepdims=False)
        my_ids = lax.dynamic_index_in_dim(incoming, own, 0, keepdims=False)
        my_hop = hop_from(replicas, own, my_place // store_rows)
        my_index = jnp.where(my_hop == 0, my_place % store_rows, my_earlier)
        replaced = evict[None, :] == jnp.arange(slots, dtype=jnp.int32)[:, None]
        is_new = jnp.any(replaced, axis=1)

        def per_slot(new, old):
            chosen = jnp.sum(jnp.where(replaced, new[None, :], 0), axis=1)
            return jnp.where(is_new, chosen, old).astype(jnp.int32)

        kind = per_slot(1 + my_hop, jnp.zeros((slots,), jnp.int32))
        place_in = per_slot(my_index, jnp.arange(slots, dtype=jnp.int32))
        ids = per_slot(my_ids, resident_ids[0])
        index = jnp.concatenate(
            [jnp.where(kind == n, place_in, 0) for n in range(1 + replicas)]
        ).astype(jnp.int32)
        wanted = req_adapter[:, None]
        sources = [resident_factors, store_factors]
        if tensor == 4:
            inner = (z == 1) | (z == 2)
            rounds = [(edges(0, 0), True), ([(1, 2), (2, 1)], True), ([(1, 0), (2, 3)], inner)]
        else:
            bits = [1 << n for n in range(tensor.bit_length() - 1)]
            rounds = [(exchange(tensor, bit)[0], True) for bit in bits]
        state = {"mine": None, "theirs": None, "keep": None}

        def fetch(after):
            if not send_rows:
                return after
            picked = pick(store_factors, jnp.concatenate(send_rows).astype(jnp.int32), after)
            for piece, (pairs, _) in reversed(list(zip(picked, hops))):
                sources.insert(2, lax.ppermute(piece, "replica", pairs))
            return picked[0]

        def send_mine():
            state["theirs"] = None
            if rounds:
                pairs, state["keep"] = rounds.pop(0)
                state["theirs"] = lax.ppermute(state["mine"], "tensor", pairs)

        def shrink(after):
            state["mine"], state["expand"] = hold_slots(
                attn_out, wanted, ids, kind, index, sources, after
            )
            if tensor & (tensor - 1) == 0:
                send_mine()
            else:
                state["mine"] = lax.psum(state["mine"], "tensor")
            return state["mine"]

        def add_theirs(after):
            if state["theirs"] is None:
                return after
            state["mine"] = join(jnp.asarray(state["keep"]), state["mine"], state["theirs"], after)
            send_mine()
            return state["mine"]

        def between(step, piece, after):
            if step == 0 and piece == len(spans(width, True)) - 1:
                return fetch(after)
            if step == 1 and piece == 0:
                return shrink(after)
            return add_theirs(after)

        came_x, came_y, last = [], [], None
        for step in range(tensor - 1):
            came_x, came_y, last = step_of(step, came_x, came_y, last, between)
        if tensor < 3:
            last = shrink(last)
        while state["theirs"] is not None:
            last = add_theirs(last)
        total = own_term(
            attn_out,
            out_weight,
            z,
            state["mine"],
            wanted,
            ids,
            state["expand"].reshape(-1, width),
            last,
        )
        out = None
        for span in spans(width, False):
            sums = [ref for at, ref in came_x + came_y if at == span]
            out = finish(total, sums, span[0] * tile, out)
        return out

    return local


def solution(mesh):
    return jax.shard_map(
        make_local(mesh.shape["replica"], mesh.shape["tensor"]),
        mesh=mesh,
        in_specs=(
            P(("groups", "replica"), "tensor"),
            P("tensor", None),
            P(("groups", "replica"), None, None, "tensor"),
            P(("groups", "replica"), None, None, "tensor"),
            P(("groups", "replica"), None),
            P(("groups", "replica"), None),
            P("groups", None),
            P("groups"),
            P(("groups", "replica")),
        ),
        out_specs=P(("groups", "replica"), "tensor"),
        check_vma=False,
    )
```

```python
import functools

import jax
import jax.numpy as jnp
from jax import lax
from jax.experimental import pallas as pl
from jax.experimental.pallas import tpu as pltpu
from jax.sharding import PartitionSpec as P

CAP = 2
FIRST = 1
ROW_PARTS = 2
VMEM = 28 * 1024 * 1024
FIRST_VMEM = 60 * 1024 * 1024
SCALE = 3.0


def cost(flops, elements):
    return pl.CostEstimate(
        flops=int(SCALE * flops), bytes_accessed=int(SCALE * 2 * elements), transcendentals=0
    )


def params(vmem=VMEM):
    return pltpu.CompilerParams(vmem_limit_bytes=vmem)


ORDER = pl.BlockSpec(memory_space=pl.ANY)


def term_kernel(ranges, place_ref, a_ref, w_ref, *rest):
    out_ref = rest[-1]
    j = pl.program_id(0)
    total = jnp.dot(a_ref[...], w_ref[...], preferred_element_type=jnp.float32)
    for n, (low, count) in enumerate(ranges):
        counts = (place_ref[1 + n] > 0) & (j >= low) & (j < low + count)
        total += jnp.where(counts, rest[n][...].astype(jnp.float32), 0.0)
    out_ref[...] = total.astype(out_ref.dtype)


def tile_of(width):
    return max(128, width // 8)


def spans(width, first):
    tiles = width // tile_of(width)
    half = tiles // 2
    shares = [half, tiles - half] if half else [tiles]
    if first and half > 2:
        shares = [FIRST, half - FIRST, tiles - half]
    return [(sum(shares[:n]), share) for n, share in enumerate(shares)]


def term(attn, weight, first_tile, tile, tiles, came, after):
    rows, depth = attn.shape
    ranges = [(low, ref.shape[1] // tile) for ref, _, low in came]

    def part_spec(low, count):
        return pl.BlockSpec((rows, tile), lambda j, b: (0, jnp.clip(j - low, 0, count - 1)))

    return pl.pallas_call(
        functools.partial(term_kernel, ranges),
        grid_spec=pltpu.PrefetchScalarGridSpec(
            num_scalar_prefetch=1,
            grid=(tiles,),
            in_specs=[
                pl.BlockSpec(memory_space=pltpu.VMEM),
                pl.BlockSpec((depth, tile), lambda j, b: (0, b[0] + j)),
            ]
            + [part_spec(*span) for span in ranges]
            + [ORDER],
            out_specs=pl.BlockSpec((rows, tile), lambda j, b: (0, j)),
        ),
        out_shape=jax.ShapeDtypeStruct((rows, tiles * tile), jnp.bfloat16),
        compiler_params=params(),
        cost_estimate=cost(2 * rows * depth * tiles * tile, depth * tiles * tile),
    )(
        jnp.stack([first_tile, *[flag for _, flag, _ in came]]).astype(jnp.int32),
        attn,
        weight,
        *[ref for ref, _, _ in came],
        after,
    )


def first_kernel(place_ref, a_ref, w_ref, out_ref, token_ref):
    total = jnp.dot(a_ref[...], w_ref[...], preferred_element_type=jnp.float32)
    out_ref[...] = total.astype(out_ref.dtype)
    token_ref[...] = jnp.zeros_like(token_ref)


def first_term(attn, weight, first_tile, tile, tiles):
    rows, depth = attn.shape
    step = rows // ROW_PARTS
    return pl.pallas_call(
        first_kernel,
        grid_spec=pltpu.PrefetchScalarGridSpec(
            num_scalar_prefetch=1,
            grid=(ROW_PARTS,),
            in_specs=[
                pl.BlockSpec((step, depth), lambda n, b: (n, 0)),
                pl.BlockSpec((depth, tiles * tile), lambda n, b: (0, b[0] // tiles)),
            ],
            out_specs=[
                pl.BlockSpec((step, tiles * tile), lambda n, b: (n, 0)),
                pl.BlockSpec((8, 128), lambda n, b: (0, 0)),
            ],
        ),
        out_shape=[
            jax.ShapeDtypeStruct((rows, tiles * tile), jnp.bfloat16),
            jax.ShapeDtypeStruct((8, 128), jnp.float32),
        ],
        compiler_params=params(FIRST_VMEM),
        cost_estimate=cost(2 * rows * depth * tiles * tile, depth * tiles * tile),
    )(first_tile.reshape(1).astype(jnp.int32), attn, weight)


def exchange(size, hop):
    if size & (size - 1) == 0:
        return [(d, d ^ hop) for d in range(size)], lambda d: d ^ hop
    return [(d, (d + hop) % size) for d in range(size)], lambda d: lax.rem(d + hop, size)


def hop_from(size, here, source):
    if size & (size - 1) == 0:
        return here ^ source
    return lax.rem(here - source + size, size)


def pick_kernel(count, row_ref, *refs):
    for n in range(count):
        refs[count + 1 + n][...] = refs[n][...]


def pick(store, rows, after):
    count = rows.shape[0] // CAP
    shape = (1,) + store.shape[1:]

    def from_spec(n):
        return pl.BlockSpec(shape, lambda c, row: (row[n * CAP + c], 0, 0, 0))

    return pl.pallas_call(
        functools.partial(pick_kernel, count),
        grid_spec=pltpu.PrefetchScalarGridSpec(
            num_scalar_prefetch=1,
            grid=(CAP,),
            in_specs=[from_spec(n) for n in range(count)] + [ORDER],
            out_specs=[pl.BlockSpec(shape, lambda c, row: (c, 0, 0, 0))] * count,
        ),
        out_shape=[jax.ShapeDtypeStruct((CAP,) + store.shape[1:], store.dtype)] * count,
        compiler_params=params(),
        cost_estimate=cost(0, 2 * rows.shape[0] * store[0].size),
    )(rows, *[store] * count, after)


def slots_kernel(count, kind_ref, index_ref, id_ref, a_ref, wanted_ref, *rest):
    from_refs = rest[:count]
    mine_ref, expand_ref, factors = rest[-3:]
    s = pl.program_id(0)
    rank = expand_ref.shape[1]
    here = pl.ds(pl.multiple_of(s * rank, rank), rank)

    for n, ref in enumerate(from_refs):

        @pl.when(kind_ref[s] == n)
        def _():
            factors[here, :] = ref[0, 0]
            expand_ref[0] = ref[0, 1]

    @pl.when(s == pl.num_programs(0) - 1)
    def _():
        shrunk = lax.dot_general(
            a_ref[...], factors[...], (((1,), (1,)), ((), ())), preferred_element_type=jnp.float32
        )
        total = jnp.zeros(mine_ref.shape, jnp.float32)
        for n in range(factors.shape[0] // rank):
            total += jnp.where(wanted_ref[...] == id_ref[n], shrunk[:, n * rank : (n + 1) * rank], 0.0)
        mine_ref[...] = total.astype(mine_ref.dtype)


def hold_slots(attn, wanted, ids, kind, index, sources, after):
    rows, depth = attn.shape
    slots = ids.shape[0]
    rank, width = sources[0].shape[2:]

    def from_spec(n):
        return pl.BlockSpec(
            (1, 2, rank, width), lambda s, kind, index, ids: (index[n * slots + s], 0, 0, 0)
        )

    return pl.pallas_call(
        functools.partial(slots_kernel, len(sources)),
        grid_spec=pltpu.PrefetchScalarGridSpec(
            num_scalar_prefetch=3,
            grid=(slots,),
            in_specs=[
                pl.BlockSpec(memory_space=pltpu.VMEM),
                pl.BlockSpec((rows, 1), lambda s, *_: (0, 0)),
            ]
            + [from_spec(n) for n in range(len(sources))]
            + [ORDER],
            out_specs=[
                pl.BlockSpec((rows, rank), lambda s, *_: (0, 0)),
                pl.BlockSpec((1, rank, width), lambda s, *_: (s, 0, 0)),
            ],
            scratch_shapes=[pltpu.VMEM((slots * rank, width), jnp.bfloat16)],
        ),
        out_shape=[
            jax.ShapeDtypeStruct((rows, rank), jnp.bfloat16),
            jax.ShapeDtypeStruct((slots, rank, width), jnp.bfloat16),
        ],
        compiler_params=params(),
        cost_estimate=cost(2 * rows * depth * slots * rank, 3 * slots * rank * width),
    )(kind, index, ids, attn, wanted, *sources, after)


def join_kernel(keep_ref, mine_ref, theirs_ref, after_ref, out_ref):
    out_ref[...] = (
        jnp.where(keep_ref[0] > 0, mine_ref[...].astype(jnp.float32), 0.0)
        + theirs_ref[...].astype(jnp.float32)
    ).astype(out_ref.dtype)


def join(keep, mine, theirs, after):
    whole = pl.BlockSpec(mine.shape, lambda: (0, 0))
    return pl.pallas_call(
        join_kernel,
        in_specs=[pl.BlockSpec(memory_space=pltpu.SMEM), whole, whole, ORDER],
        out_specs=whole,
        out_shape=jax.ShapeDtypeStruct(mine.shape, mine.dtype),
        compiler_params=params(),
        cost_estimate=cost(0, 3 * mine.size),
    )(jnp.reshape(keep, (1,)).astype(jnp.int32), mine, theirs, after)


def own_kernel(block_ref, id_ref, a_ref, w_ref, chosen_ref, wanted_ref, expand_ref, after_ref, out_ref, masked):
    @pl.when(pl.program_id(0) == 0)
    def _():
        chosen = chosen_ref[...]
        rank = chosen.shape[1]
        for n in range(masked.shape[1] // rank):
            masked[:, n * rank : (n + 1) * rank] = jnp.where(
                wanted_ref[...] == id_ref[n], chosen, jnp.zeros_like(chosen)
            )

    out_ref[...] = jnp.dot(
        a_ref[...], w_ref[...], preferred_element_type=jnp.float32
    ) + jnp.dot(masked[...], expand_ref[...], preferred_element_type=jnp.float32)


def own_term(attn, weight, block, chosen, wanted, ids, expand, after):
    rows, depth = attn.shape
    ranks, width = expand.shape
    tile = width // 4
    tiles = 4
    return pl.pallas_call(
        own_kernel,
        grid_spec=pltpu.PrefetchScalarGridSpec(
            num_scalar_prefetch=2,
            grid=(tiles,),
            in_specs=[
                pl.BlockSpec(memory_space=pltpu.VMEM),
                pl.BlockSpec((depth, tile), lambda j, b, ids: (0, b[0] * tiles + j)),
                pl.BlockSpec(chosen.shape, lambda j, *_: (0, 0)),
                pl.BlockSpec((rows, 1), lambda j, *_: (0, 0)),
                pl.BlockSpec((ranks, tile), lambda j, *_: (0, j)),
                ORDER,
            ],
            out_specs=pl.BlockSpec((rows, tile), lambda j, *_: (0, j)),
            scratch_shapes=[pltpu.VMEM((rows, ranks), jnp.bfloat16)],
        ),
        out_shape=jax.ShapeDtypeStruct((rows, width), jnp.float32),
        compiler_params=params(),
        cost_estimate=cost(2 * rows * width * (depth + ranks), (depth + ranks) * width + 2 * rows * width),
    )(block.reshape(1).astype(jnp.int32), ids, attn, weight, chosen, wanted, expand, after)


def finish_kernel(sums, own_ref, *rest):
    out_ref = rest[-1]
    total = own_ref[...]
    for ref in rest[:sums]:
        total += ref[...].astype(jnp.float32)
    out_ref[...] = total.astype(out_ref.dtype)


def finish(own, sums, first_column, so_far):
    rows, width = own.shape
    tile = tile_of(width) * 2
    here = pl.BlockSpec((rows, tile), lambda j: (0, first_column // tile + j))
    came = pl.BlockSpec((rows, tile), lambda j: (0, j))
    extra = [] if so_far is None else [so_far]
    return pl.pallas_call(
        functools.partial(finish_kernel, len(sums)),
        grid=(sums[0].shape[1] // tile,),
        in_specs=[here] + [came] * len(sums) + [pl.BlockSpec(memory_space=pl.ANY)] * len(extra),
        out_specs=here,
        out_shape=jax.ShapeDtypeStruct((rows, width), jnp.bfloat16),
        input_output_aliases={1 + len(sums): 0} if extra else {},
        compiler_params=params(),
        cost_estimate=cost(0, 5 * rows * sums[0].shape[1]),
    )(own, *sums, *extra)


def make_local(replicas, tensor):
    def local(
        attn_out,
        out_weight,
        store_factors,
        resident_factors,
        resident_ids,
        evict_slots,
        incoming,
        store_place,
        req_adapter,
    ):
        z = lax.axis_index("tensor")
        own = lax.axis_index("replica")
        width = out_weight.shape[1] // tensor
        tile = tile_of(width)
        slots = resident_factors.shape[0]
        store_rows = store_factors.shape[0]
        evict = evict_slots[0]
        even, odd = z % 2 == 0, z % 2 == 1
        not_first, not_last = z > 0, z < tensor - 1

        def edges(step, first):
            pairs = []
            for d in range(first, tensor - 1, 2):
                pairs += [(d, d + 1)] * (d <= step)
                pairs += [(d + 1, d)] * (d + 1 >= tensor - 1 - step)
            return pairs

        def swap(pairs):
            return pairs + [(b, a) for a, b in pairs if (b, a) not in pairs]

        def product(block, span, came_a, flag_a, came_b, flag_b, after):
            start, tiles = span
            first = jnp.clip(block, 0, tensor - 1) * (width // tile) + start
            if after is None:
                return first_term(attn_out, out_weight, first, tile, tiles)
            came = []
            for sums, flag in ((came_a, flag_a), (came_b, flag_b)):
                for (low, count), ref in sums:
                    if low < start + tiles and start < low + count:
                        came.append((ref, flag, low - start))
            out = term(attn_out, out_weight, first, tile, tiles, came, after)
            return out, out

        def step_of(step, came_x, came_y, after, between):
            right_block = tensor - 1 - step + z
            left_block = z + step + 1 - tensor
            pairs_x, pairs_y = edges(step, 0), edges(step, 1)
            xs, ys = [], []
            for span in spans(width, step == 0):
                if 2 * step < tensor - 1:
                    goes_right = 2 * z < tensor
                    block = jnp.where(goes_right, right_block, left_block)
                    flag_x = jnp.where(goes_right, odd, even & not_last)
                    flag_y = jnp.where(goes_right, even & not_first, odd & not_last)
                    for_x, last = product(block, span, came_x, flag_x, came_y, flag_y, after)
                    for_y = for_x
                else:
                    flag = jnp.where(even, not_first, not_last)
                    block = jnp.where(even, right_block, left_block)
                    for_x, last = product(block, span, [], flag, came_y, flag, after)
                    block = jnp.where(even, left_block, right_block)
                    for_y, last = product(block, span, came_x, flag, [], flag, last)
                pairs = pairs_x if step else swap(pairs_x)
                xs.append((span, lax.ppermute(for_x, "tensor", pairs)))
                if pairs_y:
                    ys.append((span, lax.ppermute(for_y, "tensor", pairs_y)))
                after = between(step, len(xs) - 1, last)
            return xs, ys, after

        matches = incoming[:, :, None] == jnp.arange(store_place.shape[0], dtype=jnp.int32)
        place = jnp.sum(jnp.where(matches, store_place, 0), axis=2)
        owners = place // store_rows
        spots = jnp.arange(place.shape[1], dtype=jnp.int32)
        earlier = jnp.sum(
            (owners[:, :, None] == owners[:, None, :]) & (spots[None, :] < spots[:, None]), axis=2
        ).astype(jnp.int32)
        asked = (owners == own)[:, :, None] & (
            earlier[:, :, None] == jnp.arange(CAP, dtype=jnp.int32)
        )
        rows_for = jnp.sum(jnp.where(asked, (place % store_rows)[:, :, None], 0), axis=1)
        hops = [exchange(replicas, hop) for hop in range(1, replicas)]
        send_rows = [
            lax.dynamic_index_in_dim(rows_for, to(own), 0, keepdims=False) for _, to in hops
        ]

        my_place = lax.dynamic_index_in_dim(place, own, 0, keepdims=False)
        my_earlier = lax.dynamic_index_in_dim(earlier, own, 0, keepdims=False)
        my_ids = lax.dynamic_index_in_dim(incoming, own, 0, keepdims=False)
        my_hop = hop_from(replicas, own, my_place // store_rows)
        my_index = jnp.where(my_hop == 0, my_place % store_rows, my_earlier)
        replaced = evict[None, :] == jnp.arange(slots, dtype=jnp.int32)[:, None]
        is_new = jnp.any(replaced, axis=1)

        def per_slot(new, old):
            chosen = jnp.sum(jnp.where(replaced, new[None, :], 0), axis=1)
            return jnp.where(is_new, chosen, old).astype(jnp.int32)

        kind = per_slot(1 + my_hop, jnp.zeros((slots,), jnp.int32))
        place_in = per_slot(my_index, jnp.arange(slots, dtype=jnp.int32))
        ids = per_slot(my_ids, resident_ids[0])
        index = jnp.concatenate(
            [jnp.where(kind == n, place_in, 0) for n in range(1 + replicas)]
        ).astype(jnp.int32)
        wanted = req_adapter[:, None]
        sources = [resident_factors, store_factors]
        if tensor == 4:
            inner = (z == 1) | (z == 2)
            rounds = [(edges(0, 0), True), ([(1, 2), (2, 1)], True), ([(1, 0), (2, 3)], inner)]
        else:
            bits = [1 << n for n in range(tensor.bit_length() - 1)]
            rounds = [(exchange(tensor, bit)[0], True) for bit in bits]
        state = {"mine": None, "theirs": None, "keep": None}

        def fetch(after):
            if not send_rows:
                return after
            picked = pick(store_factors, jnp.concatenate(send_rows).astype(jnp.int32), after)
            for piece, (pairs, _) in reversed(list(zip(picked, hops))):
                sources.insert(2, lax.ppermute(piece, "replica", pairs))
            return picked[0]

        def send_mine():
            state["theirs"] = None
            if rounds:
                pairs, state["keep"] = rounds.pop(0)
                state["theirs"] = lax.ppermute(state["mine"], "tensor", pairs)

        def shrink(after):
            state["mine"], state["expand"] = hold_slots(
                attn_out, wanted, ids, kind, index, sources, after
            )
            if tensor & (tensor - 1) == 0:
                send_mine()
            else:
                state["mine"] = lax.psum(state["mine"], "tensor")
            return state["mine"]

        def add_theirs(after):
            if state["theirs"] is None:
                return after
            state["mine"] = join(jnp.asarray(state["keep"]), state["mine"], state["theirs"], after)
            send_mine()
            return state["mine"]

        def between(step, piece, after):
            if step == 0 and piece == len(spans(width, True)) - 1:
                return fetch(after)
            if step == 1 and piece == 0:
                return shrink(after)
            return add_theirs(after)

        came_x, came_y, last = [], [], None
        for step in range(tensor - 1):
            came_x, came_y, last = step_of(step, came_x, came_y, last, between)
        if tensor < 3:
            last = shrink(last)
        while state["theirs"] is not None:
            last = add_theirs(last)
        total = own_term(
            attn_out,
            out_weight,
            z,
            state["mine"],
            wanted,
            ids,
            state["expand"].reshape(-1, width),
            last,
        )
        out = None
        for span in spans(width, False):
            sums = [ref for at, ref in came_x + came_y if at == span]
            out = finish(total, sums, span[0] * tile, out)
        return out

    return local


def solution(mesh):
    return jax.shard_map(
        make_local(mesh.shape["replica"], mesh.shape["tensor"]),
        mesh=mesh,
        in_specs=(
            P(("groups", "replica"), "tensor"),
            P("tensor", None),
            P(("groups", "replica"), None, None, "tensor"),
            P(("groups", "replica"), None, None, "tensor"),
            P(("groups", "replica"), None),
            P(("groups", "replica"), None),
            P("groups", None),
            P("groups"),
            P(("groups", "replica")),
        ),
        out_specs=P(("groups", "replica"), "tensor"),
        check_vma=False,
    )
```

```python
import functools
import math

import jax
import jax.numpy as jnp
from jax import lax
from jax.experimental import pallas as pl
from jax.experimental.pallas import tpu as pltpu
from jax.sharding import PartitionSpec as P

CAP = 2
FIRST = 1
LAST = 1
ROW_PARTS = 2
VMEM = 28 * 1024 * 1024
FIRST_VMEM = 60 * 1024 * 1024
SCALE = 3.0


def cost(flops, elements):
    return pl.CostEstimate(
        flops=int(SCALE * flops), bytes_accessed=int(SCALE * 2 * elements), transcendentals=0
    )


def params(vmem=VMEM):
    return pltpu.CompilerParams(vmem_limit_bytes=vmem)


ORDER = pl.BlockSpec(memory_space=pl.ANY)


def term_kernel(ranges, place_ref, a_ref, w_ref, *rest):
    out_ref = rest[-1]
    j = pl.program_id(0)
    total = jnp.dot(a_ref[...], w_ref[...], preferred_element_type=jnp.float32)
    for n, (low, count) in enumerate(ranges):
        counts = (place_ref[1 + n] > 0) & (j >= low) & (j < low + count)
        total += jnp.where(counts, rest[n][...].astype(jnp.float32), 0.0)
    out_ref[...] = total.astype(out_ref.dtype)


def tile_of(width):
    return max(128, width // 8)


def spans(width, step, steps):
    tiles = width // tile_of(width)
    half = tiles // 2
    shares = [half, tiles - half] if half else [tiles]
    if half > 2 and step == 0:
        shares = [FIRST, half - FIRST, tiles - half]
    if half > 2 and step == steps - 1:
        shares = [half, tiles - half - LAST, LAST] if LAST else shares
    return [(sum(shares[:n]), share) for n, share in enumerate(shares)]


def term(attn, weight, first_tile, tile, tiles, came, after):
    rows, depth = attn.shape
    ranges = [(low, ref.shape[1] // tile) for ref, _, low in came]

    def part_spec(low, count):
        return pl.BlockSpec((rows, tile), lambda j, b: (0, jnp.clip(j - low, 0, count - 1)))

    return pl.pallas_call(
        functools.partial(term_kernel, ranges),
        grid_spec=pltpu.PrefetchScalarGridSpec(
            num_scalar_prefetch=1,
            grid=(tiles,),
            in_specs=[
                pl.BlockSpec(memory_space=pltpu.VMEM),
                pl.BlockSpec((depth, tile), lambda j, b: (0, b[0] + j)),
            ]
            + [part_spec(*span) for span in ranges]
            + [ORDER],
            out_specs=pl.BlockSpec((rows, tile), lambda j, b: (0, j)),
        ),
        out_shape=jax.ShapeDtypeStruct((rows, tiles * tile), jnp.bfloat16),
        compiler_params=params(),
        cost_estimate=cost(2 * rows * depth * tiles * tile, depth * tiles * tile),
    )(
        jnp.stack([first_tile, *[flag for _, flag, _ in came]]).astype(jnp.int32),
        attn,
        weight,
        *[ref for ref, _, _ in came],
        after,
    )


def first_kernel(place_ref, a_ref, w_ref, out_ref, token_ref):
    total = jnp.dot(a_ref[...], w_ref[...], preferred_element_type=jnp.float32)
    out_ref[...] = total.astype(out_ref.dtype)
    token_ref[...] = jnp.zeros_like(token_ref)


def first_term(attn, weight, first_tile, tile, tiles):
    rows, depth = attn.shape
    step = rows // ROW_PARTS
    return pl.pallas_call(
        first_kernel,
        grid_spec=pltpu.PrefetchScalarGridSpec(
            num_scalar_prefetch=1,
            grid=(ROW_PARTS,),
            in_specs=[
                pl.BlockSpec((step, depth), lambda n, b: (n, 0)),
                pl.BlockSpec((depth, tiles * tile), lambda n, b: (0, b[0] // tiles)),
            ],
            out_specs=[
                pl.BlockSpec((step, tiles * tile), lambda n, b: (n, 0)),
                pl.BlockSpec((8, 128), lambda n, b: (0, 0)),
            ],
        ),
        out_shape=[
            jax.ShapeDtypeStruct((rows, tiles * tile), jnp.bfloat16),
            jax.ShapeDtypeStruct((8, 128), jnp.float32),
        ],
        compiler_params=params(FIRST_VMEM),
        cost_estimate=cost(2 * rows * depth * tiles * tile, depth * tiles * tile),
    )(first_tile.reshape(1).astype(jnp.int32), attn, weight)


def exchange(size, hop):
    if size & (size - 1) == 0:
        return [(d, d ^ hop) for d in range(size)], lambda d: d ^ hop
    return [(d, (d + hop) % size) for d in range(size)], lambda d: lax.rem(d + hop, size)


def hop_from(size, here, source):
    if size & (size - 1) == 0:
        return here ^ source
    return lax.rem(here - source + size, size)


def pick_kernel(count, row_ref, *refs):
    for n in range(count):
        refs[count + 1 + n][...] = refs[n][...]


def pick(store, rows, after):
    count = rows.shape[0] // CAP
    shape = (1,) + store.shape[1:]

    def from_spec(n):
        return pl.BlockSpec(shape, lambda c, row: (row[n * CAP + c], 0, 0, 0))

    return pl.pallas_call(
        functools.partial(pick_kernel, count),
        grid_spec=pltpu.PrefetchScalarGridSpec(
            num_scalar_prefetch=1,
            grid=(CAP,),
            in_specs=[from_spec(n) for n in range(count)] + [ORDER],
            out_specs=[pl.BlockSpec(shape, lambda c, row: (c, 0, 0, 0))] * count,
        ),
        out_shape=[jax.ShapeDtypeStruct((CAP,) + store.shape[1:], store.dtype)] * count,
        compiler_params=params(),
        cost_estimate=cost(0, 2 * rows.shape[0] * store[0].size),
    )(rows, *[store] * count, after)


def slots_kernel(count, kind_ref, index_ref, id_ref, a_ref, wanted_ref, *rest):
    from_refs = rest[:count]
    mine_ref, expand_ref, factors = rest[-3:]
    s = pl.program_id(0)
    rank = expand_ref.shape[1]
    here = pl.ds(pl.multiple_of(s * rank, rank), rank)

    for n, ref in enumerate(from_refs):

        @pl.when(kind_ref[s] == n)
        def _():
            factors[here, :] = ref[0, 0]
            expand_ref[0] = ref[0, 1]

    @pl.when(s == pl.num_programs(0) - 1)
    def _():
        shrunk = lax.dot_general(
            a_ref[...], factors[...], (((1,), (1,)), ((), ())), preferred_element_type=jnp.float32
        )
        total = jnp.zeros(mine_ref.shape, jnp.float32)
        for n in range(factors.shape[0] // rank):
            total += jnp.where(wanted_ref[...] == id_ref[n], shrunk[:, n * rank : (n + 1) * rank], 0.0)
        mine_ref[...] = total.astype(mine_ref.dtype)


def hold_slots(attn, wanted, ids, kind, index, sources, after):
    rows, depth = attn.shape
    slots = ids.shape[0]
    rank, width = sources[0].shape[2:]

    def from_spec(n):
        return pl.BlockSpec(
            (1, 2, rank, width), lambda s, kind, index, ids: (index[n * slots + s], 0, 0, 0)
        )

    return pl.pallas_call(
        functools.partial(slots_kernel, len(sources)),
        grid_spec=pltpu.PrefetchScalarGridSpec(
            num_scalar_prefetch=3,
            grid=(slots,),
            in_specs=[
                pl.BlockSpec(memory_space=pltpu.VMEM),
                pl.BlockSpec((rows, 1), lambda s, *_: (0, 0)),
            ]
            + [from_spec(n) for n in range(len(sources))]
            + [ORDER],
            out_specs=[
                pl.BlockSpec((rows, rank), lambda s, *_: (0, 0)),
                pl.BlockSpec((1, rank, width), lambda s, *_: (s, 0, 0)),
            ],
            scratch_shapes=[pltpu.VMEM((slots * rank, width), jnp.bfloat16)],
        ),
        out_shape=[
            jax.ShapeDtypeStruct((rows, rank), jnp.bfloat16),
            jax.ShapeDtypeStruct((slots, rank, width), jnp.bfloat16),
        ],
        compiler_params=params(),
        cost_estimate=cost(2 * rows * depth * slots * rank, 3 * slots * rank * width),
    )(kind, index, ids, attn, wanted, *sources, after)


def join_kernel(keep_ref, mine_ref, theirs_ref, after_ref, out_ref):
    out_ref[...] = (
        jnp.where(keep_ref[0] > 0, mine_ref[...].astype(jnp.float32), 0.0)
        + theirs_ref[...].astype(jnp.float32)
    ).astype(out_ref.dtype)


def join(keep, mine, theirs, after):
    whole = pl.BlockSpec(mine.shape, lambda: (0, 0))
    return pl.pallas_call(
        join_kernel,
        in_specs=[pl.BlockSpec(memory_space=pltpu.SMEM), whole, whole, ORDER],
        out_specs=whole,
        out_shape=jax.ShapeDtypeStruct(mine.shape, mine.dtype),
        compiler_params=params(),
        cost_estimate=cost(0, 3 * mine.size),
    )(jnp.reshape(keep, (1,)).astype(jnp.int32), mine, theirs, after)


def own_kernel(block_ref, id_ref, a_ref, w_ref, chosen_ref, wanted_ref, expand_ref, after_ref, out_ref, masked):
    @pl.when(pl.program_id(0) == 0)
    def _():
        chosen = chosen_ref[...]
        rank = chosen.shape[1]
        for n in range(masked.shape[1] // rank):
            masked[:, n * rank : (n + 1) * rank] = jnp.where(
                wanted_ref[...] == id_ref[n], chosen, jnp.zeros_like(chosen)
            )

    out_ref[...] = jnp.dot(
        a_ref[...], w_ref[...], preferred_element_type=jnp.float32
    ) + jnp.dot(masked[...], expand_ref[...], preferred_element_type=jnp.float32)


def own_term(attn, weight, block, chosen, wanted, ids, expand, after):
    rows, depth = attn.shape
    ranks, width = expand.shape
    tile = width // 4
    tiles = 4
    return pl.pallas_call(
        own_kernel,
        grid_spec=pltpu.PrefetchScalarGridSpec(
            num_scalar_prefetch=2,
            grid=(tiles,),
            in_specs=[
                pl.BlockSpec(memory_space=pltpu.VMEM),
                pl.BlockSpec((depth, tile), lambda j, b, ids: (0, b[0] * tiles + j)),
                pl.BlockSpec(chosen.shape, lambda j, *_: (0, 0)),
                pl.BlockSpec((rows, 1), lambda j, *_: (0, 0)),
                pl.BlockSpec((ranks, tile), lambda j, *_: (0, j)),
                ORDER,
            ],
            out_specs=pl.BlockSpec((rows, tile), lambda j, *_: (0, j)),
            scratch_shapes=[pltpu.VMEM((rows, ranks), jnp.bfloat16)],
        ),
        out_shape=jax.ShapeDtypeStruct((rows, width), jnp.float32),
        compiler_params=params(),
        cost_estimate=cost(2 * rows * width * (depth + ranks), (depth + ranks) * width + 2 * rows * width),
    )(block.reshape(1).astype(jnp.int32), ids, attn, weight, chosen, wanted, expand, after)


def finish_kernel(sums, own_ref, *rest):
    out_ref = rest[-1]
    total = own_ref[...]
    for ref in rest[:sums]:
        total += ref[...].astype(jnp.float32)
    out_ref[...] = total.astype(out_ref.dtype)


def finish(own, sums, first_column, so_far):
    rows, width = own.shape
    tile = math.gcd(2 * tile_of(width), sums[0].shape[1], first_column)
    here = pl.BlockSpec((rows, tile), lambda j: (0, first_column // tile + j))
    came = pl.BlockSpec((rows, tile), lambda j: (0, j))
    extra = [] if so_far is None else [so_far]
    return pl.pallas_call(
        functools.partial(finish_kernel, len(sums)),
        grid=(sums[0].shape[1] // tile,),
        in_specs=[here] + [came] * len(sums) + [pl.BlockSpec(memory_space=pl.ANY)] * len(extra),
        out_specs=here,
        out_shape=jax.ShapeDtypeStruct((rows, width), jnp.bfloat16),
        input_output_aliases={1 + len(sums): 0} if extra else {},
        compiler_params=params(),
        cost_estimate=cost(0, 5 * rows * sums[0].shape[1]),
    )(own, *sums, *extra)


def make_local(replicas, tensor):
    def local(
        attn_out,
        out_weight,
        store_factors,
        resident_factors,
        resident_ids,
        evict_slots,
        incoming,
        store_place,
        req_adapter,
    ):
        z = lax.axis_index("tensor")
        own = lax.axis_index("replica")
        width = out_weight.shape[1] // tensor
        tile = tile_of(width)
        slots = resident_factors.shape[0]
        store_rows = store_factors.shape[0]
        evict = evict_slots[0]
        even, odd = z % 2 == 0, z % 2 == 1
        not_first, not_last = z > 0, z < tensor - 1

        def edges(step, first):
            pairs = []
            for d in range(first, tensor - 1, 2):
                pairs += [(d, d + 1)] * (d <= step)
                pairs += [(d + 1, d)] * (d + 1 >= tensor - 1 - step)
            return pairs

        def swap(pairs):
            return pairs + [(b, a) for a, b in pairs if (b, a) not in pairs]

        def product(block, span, came_a, flag_a, came_b, flag_b, after):
            start, tiles = span
            first = jnp.clip(block, 0, tensor - 1) * (width // tile) + start
            if after is None:
                return first_term(attn_out, out_weight, first, tile, tiles)
            came = []
            for sums, flag in ((came_a, flag_a), (came_b, flag_b)):
                for (low, count), ref in sums:
                    if low < start + tiles and start < low + count:
                        came.append((ref, flag, low - start))
            out = term(attn_out, out_weight, first, tile, tiles, came, after)
            return out, out

        def step_of(step, came_x, came_y, after, between):
            right_block = tensor - 1 - step + z
            left_block = z + step + 1 - tensor
            pairs_x, pairs_y = edges(step, 0), edges(step, 1)
            xs, ys = [], []
            for span in spans(width, step, tensor - 1):
                if 2 * step < tensor - 1:
                    goes_right = 2 * z < tensor
                    block = jnp.where(goes_right, right_block, left_block)
                    flag_x = jnp.where(goes_right, odd, even & not_last)
                    flag_y = jnp.where(goes_right, even & not_first, odd & not_last)
                    for_x, last = product(block, span, came_x, flag_x, came_y, flag_y, after)
                    for_y = for_x
                else:
                    flag = jnp.where(even, not_first, not_last)
                    block = jnp.where(even, right_block, left_block)
                    for_x, last = product(block, span, [], flag, came_y, flag, after)
                    block = jnp.where(even, left_block, right_block)
                    for_y, last = product(block, span, came_x, flag, [], flag, last)
                pairs = pairs_x if step else swap(pairs_x)
                xs.append((span, lax.ppermute(for_x, "tensor", pairs)))
                if pairs_y:
                    ys.append((span, lax.ppermute(for_y, "tensor", pairs_y)))
                after = between(step, len(xs) - 1, last)
            return xs, ys, after

        matches = incoming[:, :, None] == jnp.arange(store_place.shape[0], dtype=jnp.int32)
        place = jnp.sum(jnp.where(matches, store_place, 0), axis=2)
        owners = place // store_rows
        spots = jnp.arange(place.shape[1], dtype=jnp.int32)
        earlier = jnp.sum(
            (owners[:, :, None] == owners[:, None, :]) & (spots[None, :] < spots[:, None]), axis=2
        ).astype(jnp.int32)
        asked = (owners == own)[:, :, None] & (
            earlier[:, :, None] == jnp.arange(CAP, dtype=jnp.int32)
        )
        rows_for = jnp.sum(jnp.where(asked, (place % store_rows)[:, :, None], 0), axis=1)
        hops = [exchange(replicas, hop) for hop in range(1, replicas)]
        send_rows = [
            lax.dynamic_index_in_dim(rows_for, to(own), 0, keepdims=False) for _, to in hops
        ]

        my_place = lax.dynamic_index_in_dim(place, own, 0, keepdims=False)
        my_earlier = lax.dynamic_index_in_dim(earlier, own, 0, keepdims=False)
        my_ids = lax.dynamic_index_in_dim(incoming, own, 0, keepdims=False)
        my_hop = hop_from(replicas, own, my_place // store_rows)
        my_index = jnp.where(my_hop == 0, my_place % store_rows, my_earlier)
        replaced = evict[None, :] == jnp.arange(slots, dtype=jnp.int32)[:, None]
        is_new = jnp.any(replaced, axis=1)

        def per_slot(new, old):
            chosen = jnp.sum(jnp.where(replaced, new[None, :], 0), axis=1)
            return jnp.where(is_new, chosen, old).astype(jnp.int32)

        kind = per_slot(1 + my_hop, jnp.zeros((slots,), jnp.int32))
        place_in = per_slot(my_index, jnp.arange(slots, dtype=jnp.int32))
        ids = per_slot(my_ids, resident_ids[0])
        index = jnp.concatenate(
            [jnp.where(kind == n, place_in, 0) for n in range(1 + replicas)]
        ).astype(jnp.int32)
        wanted = req_adapter[:, None]
        sources = [resident_factors, store_factors]
        if tensor == 4:
            inner = (z == 1) | (z == 2)
            rounds = [(edges(0, 0), True), ([(1, 2), (2, 1)], True), ([(1, 0), (2, 3)], inner)]
        else:
            bits = [1 << n for n in range(tensor.bit_length() - 1)]
            rounds = [(exchange(tensor, bit)[0], True) for bit in bits]
        state = {"mine": None, "theirs": None, "keep": None}

        def fetch(after):
            if not send_rows:
                return after
            picked = pick(store_factors, jnp.concatenate(send_rows).astype(jnp.int32), after)
            for piece, (pairs, _) in reversed(list(zip(picked, hops))):
                sources.insert(2, lax.ppermute(piece, "replica", pairs))
            return picked[0]

        def send_mine():
            state["theirs"] = None
            if rounds:
                pairs, state["keep"] = rounds.pop(0)
                state["theirs"] = lax.ppermute(state["mine"], "tensor", pairs)

        def shrink(after):
            state["mine"], state["expand"] = hold_slots(
                attn_out, wanted, ids, kind, index, sources, after
            )
            if tensor & (tensor - 1) == 0:
                send_mine()
            else:
                state["mine"] = lax.psum(state["mine"], "tensor")
            return state["mine"]

        def add_theirs(after):
            if state["theirs"] is None:
                return after
            state["mine"] = join(jnp.asarray(state["keep"]), state["mine"], state["theirs"], after)
            send_mine()
            return state["mine"]

        def between(step, piece, after):
            if step == 0 and piece == len(spans(width, 0, tensor - 1)) - 1:
                return fetch(after)
            if step == 1 and piece == 0:
                return shrink(after)
            return add_theirs(after)

        came_x, came_y, last = [], [], None
        for step in range(tensor - 1):
            came_x, came_y, last = step_of(step, came_x, came_y, last, between)
        if tensor < 3:
            last = shrink(last)
        while state["theirs"] is not None:
            last = add_theirs(last)
        total = own_term(
            attn_out,
            out_weight,
            z,
            state["mine"],
            wanted,
            ids,
            state["expand"].reshape(-1, width),
            last,
        )
        out = None
        for span in spans(width, tensor - 2, tensor - 1):
            sums = [ref for at, ref in came_x + came_y if at == span]
            out = finish(total, sums, span[0] * tile, out)
        return out

    return local


def solution(mesh):
    return jax.shard_map(
        make_local(mesh.shape["replica"], mesh.shape["tensor"]),
        mesh=mesh,
        in_specs=(
            P(("groups", "replica"), "tensor"),
            P("tensor", None),
            P(("groups", "replica"), None, None, "tensor"),
            P(("groups", "replica"), None, None, "tensor"),
            P(("groups", "replica"), None),
            P(("groups", "replica"), None),
            P("groups", None),
            P("groups"),
            P(("groups", "replica")),
        ),
        out_specs=P(("groups", "replica"), "tensor"),
        check_vma=False,
    )
```

```python
import functools
import math

import jax
import jax.numpy as jnp
from jax import lax
from jax.experimental import pallas as pl
from jax.experimental.pallas import tpu as pltpu
from jax.sharding import PartitionSpec as P

CAP = 2
FIRST = 1
LAST = 1
ROW_PARTS = 2
VMEM = 28 * 1024 * 1024
FIRST_VMEM = 60 * 1024 * 1024
SCALE = 3.0


def cost(flops, elements):
    return pl.CostEstimate(
        flops=int(SCALE * flops), bytes_accessed=int(SCALE * 2 * elements), transcendentals=0
    )


def params(vmem=VMEM):
    return pltpu.CompilerParams(vmem_limit_bytes=vmem)


ORDER = pl.BlockSpec(memory_space=pl.ANY)


def term_kernel(ranges, place_ref, a_ref, w_ref, *rest):
    out_ref = rest[-1]
    j = pl.program_id(0)
    total = jnp.dot(a_ref[...], w_ref[...], preferred_element_type=jnp.float32)
    for n, (low, count) in enumerate(ranges):
        counts = (place_ref[1 + n] > 0) & (j >= low) & (j < low + count)
        total += jnp.where(counts, rest[n][...].astype(jnp.float32), 0.0)
    out_ref[...] = total.astype(out_ref.dtype)


def tile_of(width):
    return max(128, width // 8)


def spans(width, step, steps):
    tiles = width // tile_of(width)
    half = tiles // 2
    shares = [half, tiles - half] if half else [tiles]
    if half > 2 and step == 0:
        shares = [FIRST, half - FIRST, tiles - half]
    if half > 2 and step == steps - 1:
        shares = [half, tiles - half - LAST, LAST] if LAST else shares
    return [(sum(shares[:n]), share) for n, share in enumerate(shares)]


def term(attn, weight, first_tile, tile, tiles, came, after):
    rows, depth = attn.shape
    ranges = [(low, ref.shape[1] // tile) for ref, _, low in came]

    def part_spec(low, count):
        return pl.BlockSpec((rows, tile), lambda j, b: (0, jnp.clip(j - low, 0, count - 1)))

    return pl.pallas_call(
        functools.partial(term_kernel, ranges),
        grid_spec=pltpu.PrefetchScalarGridSpec(
            num_scalar_prefetch=1,
            grid=(tiles,),
            in_specs=[
                pl.BlockSpec(memory_space=pltpu.VMEM),
                pl.BlockSpec((depth, tile), lambda j, b: (0, b[0] + j)),
            ]
            + [part_spec(*span) for span in ranges]
            + [ORDER],
            out_specs=pl.BlockSpec((rows, tile), lambda j, b: (0, j)),
        ),
        out_shape=jax.ShapeDtypeStruct((rows, tiles * tile), jnp.bfloat16),
        compiler_params=params(),
        cost_estimate=cost(2 * rows * depth * tiles * tile, depth * tiles * tile),
    )(
        jnp.stack([first_tile, *[flag for _, flag, _ in came]]).astype(jnp.int32),
        attn,
        weight,
        *[ref for ref, _, _ in came],
        after,
    )


def first_kernel(place_ref, a_ref, w_ref, out_ref, token_ref):
    total = jnp.dot(a_ref[...], w_ref[...], preferred_element_type=jnp.float32)
    out_ref[...] = total.astype(out_ref.dtype)
    token_ref[...] = jnp.zeros_like(token_ref)


def first_term(attn, weight, first_tile, tile, tiles):
    rows, depth = attn.shape
    step = rows // ROW_PARTS
    return pl.pallas_call(
        first_kernel,
        grid_spec=pltpu.PrefetchScalarGridSpec(
            num_scalar_prefetch=1,
            grid=(ROW_PARTS,),
            in_specs=[
                pl.BlockSpec((step, depth), lambda n, b: (n, 0)),
                pl.BlockSpec((depth, tiles * tile), lambda n, b: (0, b[0] // tiles)),
            ],
            out_specs=[
                pl.BlockSpec((step, tiles * tile), lambda n, b: (n, 0)),
                pl.BlockSpec((8, 128), lambda n, b: (0, 0)),
            ],
        ),
        out_shape=[
            jax.ShapeDtypeStruct((rows, tiles * tile), jnp.bfloat16),
            jax.ShapeDtypeStruct((8, 128), jnp.float32),
        ],
        compiler_params=params(FIRST_VMEM),
        cost_estimate=cost(2 * rows * depth * tiles * tile, depth * tiles * tile),
    )(first_tile.reshape(1).astype(jnp.int32), attn, weight)


def exchange(size, hop):
    if size & (size - 1) == 0:
        return [(d, d ^ hop) for d in range(size)], lambda d: d ^ hop
    return [(d, (d + hop) % size) for d in range(size)], lambda d: lax.rem(d + hop, size)


def hop_from(size, here, source):
    if size & (size - 1) == 0:
        return here ^ source
    return lax.rem(here - source + size, size)


def pick_kernel(count, row_ref, *refs):
    for n in range(count):
        refs[count + 1 + n][...] = refs[n][...]


def pick(store, rows, after):
    count = rows.shape[0] // CAP
    shape = (1,) + store.shape[1:]

    def from_spec(n):
        return pl.BlockSpec(shape, lambda c, row: (row[n * CAP + c], 0, 0, 0))

    return pl.pallas_call(
        functools.partial(pick_kernel, count),
        grid_spec=pltpu.PrefetchScalarGridSpec(
            num_scalar_prefetch=1,
            grid=(CAP,),
            in_specs=[from_spec(n) for n in range(count)] + [ORDER],
            out_specs=[pl.BlockSpec(shape, lambda c, row: (c, 0, 0, 0))] * count,
        ),
        out_shape=[jax.ShapeDtypeStruct((CAP,) + store.shape[1:], store.dtype)] * count,
        compiler_params=params(),
        cost_estimate=cost(0, 2 * rows.shape[0] * store[0].size),
    )(rows, *[store] * count, after)


def packed(values, rows):
    parts = [values[n : n + rows] for n in range(0, values.shape[0], rows)]
    return jnp.concatenate(parts, axis=1)


def unpacked(values, columns):
    parts = [values[:, n : n + columns] for n in range(0, values.shape[1], columns)]
    return jnp.concatenate(parts, axis=0)


def slots_kernel(count, kind_ref, index_ref, id_ref, a_ref, wanted_ref, *rest):
    from_refs = rest[:count]
    mine_ref, expand_ref, factors = rest[-3:]
    s = pl.program_id(0)
    rank = expand_ref.shape[1]
    here = pl.ds(pl.multiple_of(s * rank, rank), rank)

    for n, ref in enumerate(from_refs):

        @pl.when(kind_ref[s] == n)
        def _():
            factors[here, :] = ref[0, 0]
            expand_ref[0] = ref[0, 1]

    @pl.when(s == pl.num_programs(0) - 1)
    def _():
        shrunk = lax.dot_general(
            a_ref[...], factors[...], (((1,), (1,)), ((), ())), preferred_element_type=jnp.float32
        )
        total = jnp.zeros((a_ref.shape[0], rank), jnp.float32)
        for n in range(factors.shape[0] // rank):
            total += jnp.where(wanted_ref[...] == id_ref[n], shrunk[:, n * rank : (n + 1) * rank], 0.0)
        mine_ref[...] = packed(total.astype(mine_ref.dtype), mine_ref.shape[0])


def hold_slots(attn, wanted, ids, kind, index, sources, after):
    rows, depth = attn.shape
    slots = ids.shape[0]
    rank, width = sources[0].shape[2:]
    beside = max(1, 128 // rank)
    small = (rows // beside, rank * beside)

    def from_spec(n):
        return pl.BlockSpec(
            (1, 2, rank, width), lambda s, kind, index, ids: (index[n * slots + s], 0, 0, 0)
        )

    return pl.pallas_call(
        functools.partial(slots_kernel, len(sources)),
        grid_spec=pltpu.PrefetchScalarGridSpec(
            num_scalar_prefetch=3,
            grid=(slots,),
            in_specs=[
                pl.BlockSpec(memory_space=pltpu.VMEM),
                pl.BlockSpec((rows, 1), lambda s, *_: (0, 0)),
            ]
            + [from_spec(n) for n in range(len(sources))]
            + [ORDER],
            out_specs=[
                pl.BlockSpec(small, lambda s, *_: (0, 0)),
                pl.BlockSpec((1, rank, width), lambda s, *_: (s, 0, 0)),
            ],
            scratch_shapes=[pltpu.VMEM((slots * rank, width), jnp.bfloat16)],
        ),
        out_shape=[
            jax.ShapeDtypeStruct(small, jnp.bfloat16),
            jax.ShapeDtypeStruct((slots, rank, width), jnp.bfloat16),
        ],
        compiler_params=params(),
        cost_estimate=cost(2 * rows * depth * slots * rank, 3 * slots * rank * width),
    )(kind, index, ids, attn, wanted, *sources, after)


def join_kernel(keep_ref, mine_ref, theirs_ref, after_ref, out_ref):
    out_ref[...] = (
        jnp.where(keep_ref[0] > 0, mine_ref[...].astype(jnp.float32), 0.0)
        + theirs_ref[...].astype(jnp.float32)
    ).astype(out_ref.dtype)


def join(keep, mine, theirs, after):
    whole = pl.BlockSpec(mine.shape, lambda: (0, 0))
    return pl.pallas_call(
        join_kernel,
        in_specs=[pl.BlockSpec(memory_space=pltpu.SMEM), whole, whole, ORDER],
        out_specs=whole,
        out_shape=jax.ShapeDtypeStruct(mine.shape, mine.dtype),
        compiler_params=params(),
        cost_estimate=cost(0, 3 * mine.size),
    )(jnp.reshape(keep, (1,)).astype(jnp.int32), mine, theirs, after)


def own_kernel(block_ref, id_ref, a_ref, w_ref, chosen_ref, wanted_ref, expand_ref, after_ref, out_ref, masked):
    @pl.when(pl.program_id(0) == 0)
    def _():
        rank = chosen_ref.size // wanted_ref.shape[0]
        chosen = unpacked(chosen_ref[...], rank)
        for n in range(masked.shape[1] // rank):
            masked[:, n * rank : (n + 1) * rank] = jnp.where(
                wanted_ref[...] == id_ref[n], chosen, jnp.zeros_like(chosen)
            )

    out_ref[...] = jnp.dot(
        a_ref[...], w_ref[...], preferred_element_type=jnp.float32
    ) + jnp.dot(masked[...], expand_ref[...], preferred_element_type=jnp.float32)


def own_term(attn, weight, block, chosen, wanted, ids, expand, after):
    rows, depth = attn.shape
    ranks, width = expand.shape
    tile = width // 4
    tiles = 4
    return pl.pallas_call(
        own_kernel,
        grid_spec=pltpu.PrefetchScalarGridSpec(
            num_scalar_prefetch=2,
            grid=(tiles,),
            in_specs=[
                pl.BlockSpec(memory_space=pltpu.VMEM),
                pl.BlockSpec((depth, tile), lambda j, b, ids: (0, b[0] * tiles + j)),
                pl.BlockSpec(chosen.shape, lambda j, *_: (0, 0)),
                pl.BlockSpec((rows, 1), lambda j, *_: (0, 0)),
                pl.BlockSpec((ranks, tile), lambda j, *_: (0, j)),
                ORDER,
            ],
            out_specs=pl.BlockSpec((rows, tile), lambda j, *_: (0, j)),
            scratch_shapes=[pltpu.VMEM((rows, ranks), jnp.bfloat16)],
        ),
        out_shape=jax.ShapeDtypeStruct((rows, width), jnp.float32),
        compiler_params=params(),
        cost_estimate=cost(2 * rows * width * (depth + ranks), (depth + ranks) * width + 2 * rows * width),
    )(block.reshape(1).astype(jnp.int32), ids, attn, weight, chosen, wanted, expand, after)


def finish_kernel(sums, own_ref, *rest):
    out_ref = rest[-1]
    total = own_ref[...]
    for ref in rest[:sums]:
        total += ref[...].astype(jnp.float32)
    out_ref[...] = total.astype(out_ref.dtype)


def finish(own, sums, first_column, so_far):
    rows, width = own.shape
    tile = math.gcd(2 * tile_of(width), sums[0].shape[1], first_column)
    here = pl.BlockSpec((rows, tile), lambda j: (0, first_column // tile + j))
    came = pl.BlockSpec((rows, tile), lambda j: (0, j))
    extra = [] if so_far is None else [so_far]
    return pl.pallas_call(
        functools.partial(finish_kernel, len(sums)),
        grid=(sums[0].shape[1] // tile,),
        in_specs=[here] + [came] * len(sums) + [pl.BlockSpec(memory_space=pl.ANY)] * len(extra),
        out_specs=here,
        out_shape=jax.ShapeDtypeStruct((rows, width), jnp.bfloat16),
        input_output_aliases={1 + len(sums): 0} if extra else {},
        compiler_params=params(),
        cost_estimate=cost(0, 5 * rows * sums[0].shape[1]),
    )(own, *sums, *extra)


def make_local(replicas, tensor):
    def local(
        attn_out,
        out_weight,
        store_factors,
        resident_factors,
        resident_ids,
        evict_slots,
        incoming,
        store_place,
        req_adapter,
    ):
        z = lax.axis_index("tensor")
        own = lax.axis_index("replica")
        width = out_weight.shape[1] // tensor
        tile = tile_of(width)
        slots = resident_factors.shape[0]
        store_rows = store_factors.shape[0]
        evict = evict_slots[0]
        even, odd = z % 2 == 0, z % 2 == 1
        not_first, not_last = z > 0, z < tensor - 1

        def edges(step, first):
            pairs = []
            for d in range(first, tensor - 1, 2):
                pairs += [(d, d + 1)] * (d <= step)
                pairs += [(d + 1, d)] * (d + 1 >= tensor - 1 - step)
            return pairs

        def swap(pairs):
            return pairs + [(b, a) for a, b in pairs if (b, a) not in pairs]

        def product(block, span, came_a, flag_a, came_b, flag_b, after):
            start, tiles = span
            first = jnp.clip(block, 0, tensor - 1) * (width // tile) + start
            if after is None:
                return first_term(attn_out, out_weight, first, tile, tiles)
            came = []
            for sums, flag in ((came_a, flag_a), (came_b, flag_b)):
                for (low, count), ref in sums:
                    if low < start + tiles and start < low + count:
                        came.append((ref, flag, low - start))
            out = term(attn_out, out_weight, first, tile, tiles, came, after)
            return out, out

        def step_of(step, came_x, came_y, after, between):
            right_block = tensor - 1 - step + z
            left_block = z + step + 1 - tensor
            pairs_x, pairs_y = edges(step, 0), edges(step, 1)
            xs, ys = [], []
            for span in spans(width, step, tensor - 1):
                if 2 * step < tensor - 1:
                    goes_right = 2 * z < tensor
                    block = jnp.where(goes_right, right_block, left_block)
                    flag_x = jnp.where(goes_right, odd, even & not_last)
                    flag_y = jnp.where(goes_right, even & not_first, odd & not_last)
                    for_x, last = product(block, span, came_x, flag_x, came_y, flag_y, after)
                    for_y = for_x
                else:
                    flag = jnp.where(even, not_first, not_last)
                    block = jnp.where(even, right_block, left_block)
                    for_x, last = product(block, span, [], flag, came_y, flag, after)
                    block = jnp.where(even, left_block, right_block)
                    for_y, last = product(block, span, came_x, flag, [], flag, last)
                pairs = pairs_x if step else swap(pairs_x)
                xs.append((span, lax.ppermute(for_x, "tensor", pairs)))
                if pairs_y:
                    ys.append((span, lax.ppermute(for_y, "tensor", pairs_y)))
                after = between(step, len(xs) - 1, last)
            return xs, ys, after

        matches = incoming[:, :, None] == jnp.arange(store_place.shape[0], dtype=jnp.int32)
        place = jnp.sum(jnp.where(matches, store_place, 0), axis=2)
        owners = place // store_rows
        spots = jnp.arange(place.shape[1], dtype=jnp.int32)
        earlier = jnp.sum(
            (owners[:, :, None] == owners[:, None, :]) & (spots[None, :] < spots[:, None]), axis=2
        ).astype(jnp.int32)
        asked = (owners == own)[:, :, None] & (
            earlier[:, :, None] == jnp.arange(CAP, dtype=jnp.int32)
        )
        rows_for = jnp.sum(jnp.where(asked, (place % store_rows)[:, :, None], 0), axis=1)
        hops = [exchange(replicas, hop) for hop in range(1, replicas)]
        send_rows = [
            lax.dynamic_index_in_dim(rows_for, to(own), 0, keepdims=False) for _, to in hops
        ]

        my_place = lax.dynamic_index_in_dim(place, own, 0, keepdims=False)
        my_earlier = lax.dynamic_index_in_dim(earlier, own, 0, keepdims=False)
        my_ids = lax.dynamic_index_in_dim(incoming, own, 0, keepdims=False)
        my_hop = hop_from(replicas, own, my_place // store_rows)
        my_index = jnp.where(my_hop == 0, my_place % store_rows, my_earlier)
        replaced = evict[None, :] == jnp.arange(slots, dtype=jnp.int32)[:, None]
        is_new = jnp.any(replaced, axis=1)

        def per_slot(new, old):
            chosen = jnp.sum(jnp.where(replaced, new[None, :], 0), axis=1)
            return jnp.where(is_new, chosen, old).astype(jnp.int32)

        kind = per_slot(1 + my_hop, jnp.zeros((slots,), jnp.int32))
        place_in = per_slot(my_index, jnp.arange(slots, dtype=jnp.int32))
        ids = per_slot(my_ids, resident_ids[0])
        index = jnp.concatenate(
            [jnp.where(kind == n, place_in, 0) for n in range(1 + replicas)]
        ).astype(jnp.int32)
        wanted = req_adapter[:, None]
        sources = [resident_factors, store_factors]
        if tensor == 4:
            inner = (z == 1) | (z == 2)
            rounds = [(edges(0, 0), True), ([(1, 2), (2, 1)], True), ([(1, 0), (2, 3)], inner)]
        else:
            bits = [1 << n for n in range(tensor.bit_length() - 1)]
            rounds = [(exchange(tensor, bit)[0], True) for bit in bits]
        state = {"mine": None, "theirs": None, "keep": None}

        def fetch(after):
            if not send_rows:
                return after
            picked = pick(store_factors, jnp.concatenate(send_rows).astype(jnp.int32), after)
            for piece, (pairs, _) in reversed(list(zip(picked, hops))):
                sources.insert(2, lax.ppermute(piece, "replica", pairs))
            return picked[0]

        def send_mine():
            state["theirs"] = None
            if rounds:
                pairs, state["keep"] = rounds.pop(0)
                state["theirs"] = lax.ppermute(state["mine"], "tensor", pairs)

        def shrink(after):
            state["mine"], state["expand"] = hold_slots(
                attn_out, wanted, ids, kind, index, sources, after
            )
            if tensor & (tensor - 1) == 0:
                send_mine()
            else:
                state["mine"] = lax.psum(state["mine"], "tensor")
            return state["mine"]

        def add_theirs(after):
            if state["theirs"] is None:
                return after
            state["mine"] = join(jnp.asarray(state["keep"]), state["mine"], state["theirs"], after)
            send_mine()
            return state["mine"]

        def between(step, piece, after):
            if step == 0 and piece == len(spans(width, 0, tensor - 1)) - 1:
                return fetch(after)
            if step == 1 and piece == 0:
                return shrink(after)
            return add_theirs(after)

        came_x, came_y, last = [], [], None
        for step in range(tensor - 1):
            came_x, came_y, last = step_of(step, came_x, came_y, last, between)
        if tensor < 3:
            last = shrink(last)
        while state["theirs"] is not None:
            last = add_theirs(last)
        total = own_term(
            attn_out,
            out_weight,
            z,
            state["mine"],
            wanted,
            ids,
            state["expand"].reshape(-1, width),
            last,
        )
        out = None
        for span in spans(width, tensor - 2, tensor - 1):
            sums = [ref for at, ref in came_x + came_y if at == span]
            out = finish(total, sums, span[0] * tile, out)
        return out

    return local


def solution(mesh):
    return jax.shard_map(
        make_local(mesh.shape["replica"], mesh.shape["tensor"]),
        mesh=mesh,
        in_specs=(
            P(("groups", "replica"), "tensor"),
            P("tensor", None),
            P(("groups", "replica"), None, None, "tensor"),
            P(("groups", "replica"), None, None, "tensor"),
            P(("groups", "replica"), None),
            P(("groups", "replica"), None),
            P("groups", None),
            P("groups"),
            P(("groups", "replica")),
        ),
        out_specs=P(("groups", "replica"), "tensor"),
        check_vma=False,
    )
```

```python
import functools
import math

import jax
import jax.numpy as jnp
from jax import lax
from jax.experimental import pallas as pl
from jax.experimental.pallas import tpu as pltpu
from jax.sharding import PartitionSpec as P

CAP = 2
FIRST = 1
LAST = 1
ROW_PARTS = 2
VMEM = 28 * 1024 * 1024
FIRST_VMEM = 60 * 1024 * 1024
SCALE = 3.0


def cost(flops, elements):
    return pl.CostEstimate(
        flops=int(SCALE * flops), bytes_accessed=int(SCALE * 2 * elements), transcendentals=0
    )


def params(vmem=VMEM):
    return pltpu.CompilerParams(vmem_limit_bytes=vmem)


ORDER = pl.BlockSpec(memory_space=pl.ANY)


def term_kernel(ranges, place_ref, a_ref, w_ref, *rest):
    out_ref = rest[-1]
    j = pl.program_id(0)
    total = jnp.dot(a_ref[...], w_ref[...], preferred_element_type=jnp.float32)
    for n, (low, count) in enumerate(ranges):
        counts = (place_ref[1 + n] > 0) & (j >= low) & (j < low + count)
        total += jnp.where(counts, rest[n][...].astype(jnp.float32), 0.0)
    out_ref[...] = total.astype(out_ref.dtype)


def tile_of(width):
    return max(128, width // 8)


def spans(width, step, steps):
    tiles = width // tile_of(width)
    half = tiles // 2
    shares = [half, tiles - half] if half else [tiles]
    if half > 2 and step == 0:
        shares = [FIRST, half - FIRST, tiles - half]
    if half > 2 and step == steps - 1:
        shares = [half, tiles - half - LAST, LAST] if LAST else shares
    return [(sum(shares[:n]), share) for n, share in enumerate(shares)]


def term(attn, weight, first_tile, tile, tiles, came, after):
    rows, depth = attn.shape
    ranges = [(low, ref.shape[1] // tile) for ref, _, low in came]

    def part_spec(low, count):
        return pl.BlockSpec((rows, tile), lambda j, b: (0, jnp.clip(j - low, 0, count - 1)))

    return pl.pallas_call(
        functools.partial(term_kernel, ranges),
        grid_spec=pltpu.PrefetchScalarGridSpec(
            num_scalar_prefetch=1,
            grid=(tiles,),
            in_specs=[
                pl.BlockSpec(memory_space=pltpu.VMEM),
                pl.BlockSpec((depth, tile), lambda j, b: (0, b[0] + j)),
            ]
            + [part_spec(*span) for span in ranges]
            + [ORDER],
            out_specs=pl.BlockSpec((rows, tile), lambda j, b: (0, j)),
        ),
        out_shape=jax.ShapeDtypeStruct((rows, tiles * tile), jnp.bfloat16),
        compiler_params=params(),
        cost_estimate=cost(2 * rows * depth * tiles * tile, depth * tiles * tile),
    )(
        jnp.stack([first_tile, *[flag for _, flag, _ in came]]).astype(jnp.int32),
        attn,
        weight,
        *[ref for ref, _, _ in came],
        after,
    )


def first_kernel(tensor, at_ref, a_ref, w_ref, out_ref, token_ref):
    sends = (at_ref[0] == 0) | (at_ref[0] == tensor - 1)

    @pl.when(jnp.logical_not(sends))
    def _():
        out_ref[...] = jnp.zeros_like(out_ref)

    @pl.when(sends)
    def _():
        total = jnp.dot(a_ref[...], w_ref[...], preferred_element_type=jnp.float32)
        out_ref[...] = total.astype(out_ref.dtype)

    token_ref[...] = jnp.zeros_like(token_ref)


def first_term(attn, weight, z, tensor, tile, tiles):
    rows, depth = attn.shape
    last_block = (tensor - 1) * (weight.shape[1] // tensor // (tiles * tile))
    step = rows // ROW_PARTS
    return pl.pallas_call(
        functools.partial(first_kernel, tensor),
        grid_spec=pltpu.PrefetchScalarGridSpec(
            num_scalar_prefetch=1,
            grid=(ROW_PARTS,),
            in_specs=[
                pl.BlockSpec((step, depth), lambda n, at: (jnp.where((at[0] == 0) | (at[0] == tensor - 1), n, 0), 0)),
                pl.BlockSpec((depth, tiles * tile), lambda n, at: (0, jnp.where(2 * at[0] < tensor, last_block, 0))),
            ],
            out_specs=[
                pl.BlockSpec((step, tiles * tile), lambda n, b: (n, 0)),
                pl.BlockSpec((8, 128), lambda n, b: (0, 0)),
            ],
        ),
        out_shape=[
            jax.ShapeDtypeStruct((rows, tiles * tile), jnp.bfloat16),
            jax.ShapeDtypeStruct((8, 128), jnp.float32),
        ],
        compiler_params=params(FIRST_VMEM),
        cost_estimate=cost(2 * rows * depth * tiles * tile, depth * tiles * tile),
    )(z.reshape(1).astype(jnp.int32), attn, weight)


def exchange(size, hop):
    if size & (size - 1) == 0:
        return [(d, d ^ hop) for d in range(size)], lambda d: d ^ hop
    return [(d, (d + hop) % size) for d in range(size)], lambda d: lax.rem(d + hop, size)


def hop_from(size, here, source):
    if size & (size - 1) == 0:
        return here ^ source
    return lax.rem(here - source + size, size)


def pick_kernel(count, row_ref, *refs):
    for n in range(count):
        refs[count + 1 + n][...] = refs[n][...]


def pick(store, rows, after):
    count = rows.shape[0] // CAP
    shape = (1,) + store.shape[1:]

    def from_spec(n):
        return pl.BlockSpec(shape, lambda c, row: (row[n * CAP + c], 0, 0, 0))

    return pl.pallas_call(
        functools.partial(pick_kernel, count),
        grid_spec=pltpu.PrefetchScalarGridSpec(
            num_scalar_prefetch=1,
            grid=(CAP,),
            in_specs=[from_spec(n) for n in range(count)] + [ORDER],
            out_specs=[pl.BlockSpec(shape, lambda c, row: (c, 0, 0, 0))] * count,
        ),
        out_shape=[jax.ShapeDtypeStruct((CAP,) + store.shape[1:], store.dtype)] * count,
        compiler_params=params(),
        cost_estimate=cost(0, 2 * rows.shape[0] * store[0].size),
    )(rows, *[store] * count, after)


def packed(values, rows):
    parts = [values[n : n + rows] for n in range(0, values.shape[0], rows)]
    return jnp.concatenate(parts, axis=1)


def unpacked(values, columns):
    parts = [values[:, n : n + columns] for n in range(0, values.shape[1], columns)]
    return jnp.concatenate(parts, axis=0)


def slots_kernel(count, kind_ref, index_ref, id_ref, a_ref, wanted_ref, *rest):
    from_refs = rest[:count]
    mine_ref, expand_ref, factors = rest[-3:]
    s = pl.program_id(0)
    rank = expand_ref.shape[1]
    here = pl.ds(pl.multiple_of(s * rank, rank), rank)

    for n, ref in enumerate(from_refs):

        @pl.when(kind_ref[s] == n)
        def _():
            factors[here, :] = ref[0, 0]
            expand_ref[0] = ref[0, 1]

    @pl.when(s == pl.num_programs(0) - 1)
    def _():
        shrunk = lax.dot_general(
            a_ref[...], factors[...], (((1,), (1,)), ((), ())), preferred_element_type=jnp.float32
        )
        total = jnp.zeros((a_ref.shape[0], rank), jnp.float32)
        for n in range(factors.shape[0] // rank):
            total += jnp.where(wanted_ref[...] == id_ref[n], shrunk[:, n * rank : (n + 1) * rank], 0.0)
        mine_ref[...] = packed(total.astype(mine_ref.dtype), mine_ref.shape[0])


def hold_slots(attn, wanted, ids, kind, index, sources, after):
    rows, depth = attn.shape
    slots = ids.shape[0]
    rank, width = sources[0].shape[2:]
    beside = max(1, 128 // rank)
    small = (rows // beside, rank * beside)

    def from_spec(n):
        return pl.BlockSpec(
            (1, 2, rank, width), lambda s, kind, index, ids: (index[n * slots + s], 0, 0, 0)
        )

    return pl.pallas_call(
        functools.partial(slots_kernel, len(sources)),
        grid_spec=pltpu.PrefetchScalarGridSpec(
            num_scalar_prefetch=3,
            grid=(slots,),
            in_specs=[
                pl.BlockSpec(memory_space=pltpu.VMEM),
                pl.BlockSpec((rows, 1), lambda s, *_: (0, 0)),
            ]
            + [from_spec(n) for n in range(len(sources))]
            + [ORDER],
            out_specs=[
                pl.BlockSpec(small, lambda s, *_: (0, 0)),
                pl.BlockSpec((1, rank, width), lambda s, *_: (s, 0, 0)),
            ],
            scratch_shapes=[pltpu.VMEM((slots * rank, width), jnp.bfloat16)],
        ),
        out_shape=[
            jax.ShapeDtypeStruct(small, jnp.bfloat16),
            jax.ShapeDtypeStruct((slots, rank, width), jnp.bfloat16),
        ],
        compiler_params=params(),
        cost_estimate=cost(2 * rows * depth * slots * rank, 3 * slots * rank * width),
    )(kind, index, ids, attn, wanted, *sources, after)


def join_kernel(keep_ref, mine_ref, theirs_ref, after_ref, out_ref):
    out_ref[...] = (
        jnp.where(keep_ref[0] > 0, mine_ref[...].astype(jnp.float32), 0.0)
        + theirs_ref[...].astype(jnp.float32)
    ).astype(out_ref.dtype)


def join(keep, mine, theirs, after):
    whole = pl.BlockSpec(mine.shape, lambda: (0, 0))
    return pl.pallas_call(
        join_kernel,
        in_specs=[pl.BlockSpec(memory_space=pltpu.SMEM), whole, whole, ORDER],
        out_specs=whole,
        out_shape=jax.ShapeDtypeStruct(mine.shape, mine.dtype),
        compiler_params=params(),
        cost_estimate=cost(0, 3 * mine.size),
    )(jnp.reshape(keep, (1,)).astype(jnp.int32), mine, theirs, after)


def own_kernel(block_ref, id_ref, a_ref, w_ref, chosen_ref, wanted_ref, expand_ref, after_ref, out_ref, masked):
    @pl.when(pl.program_id(0) == 0)
    def _():
        rank = chosen_ref.size // wanted_ref.shape[0]
        chosen = unpacked(chosen_ref[...], rank)
        for n in range(masked.shape[1] // rank):
            masked[:, n * rank : (n + 1) * rank] = jnp.where(
                wanted_ref[...] == id_ref[n], chosen, jnp.zeros_like(chosen)
            )

    out_ref[...] = jnp.dot(
        a_ref[...], w_ref[...], preferred_element_type=jnp.float32
    ) + jnp.dot(masked[...], expand_ref[...], preferred_element_type=jnp.float32)


def own_term(attn, weight, block, chosen, wanted, ids, expand, after):
    rows, depth = attn.shape
    ranks, width = expand.shape
    tile = width // 4
    tiles = 4
    return pl.pallas_call(
        own_kernel,
        grid_spec=pltpu.PrefetchScalarGridSpec(
            num_scalar_prefetch=2,
            grid=(tiles,),
            in_specs=[
                pl.BlockSpec(memory_space=pltpu.VMEM),
                pl.BlockSpec((depth, tile), lambda j, b, ids: (0, b[0] * tiles + j)),
                pl.BlockSpec(chosen.shape, lambda j, *_: (0, 0)),
                pl.BlockSpec((rows, 1), lambda j, *_: (0, 0)),
                pl.BlockSpec((ranks, tile), lambda j, *_: (0, j)),
                ORDER,
            ],
            out_specs=pl.BlockSpec((rows, tile), lambda j, *_: (0, j)),
            scratch_shapes=[pltpu.VMEM((rows, ranks), jnp.bfloat16)],
        ),
        out_shape=jax.ShapeDtypeStruct((rows, width), jnp.float32),
        compiler_params=params(),
        cost_estimate=cost(2 * rows * width * (depth + ranks), (depth + ranks) * width + 2 * rows * width),
    )(block.reshape(1).astype(jnp.int32), ids, attn, weight, chosen, wanted, expand, after)


def finish_kernel(sums, own_ref, *rest):
    out_ref = rest[-1]
    total = own_ref[...]
    for ref in rest[:sums]:
        total += ref[...].astype(jnp.float32)
    out_ref[...] = total.astype(out_ref.dtype)


def finish(own, sums, first_column, so_far):
    rows, width = own.shape
    tile = math.gcd(2 * tile_of(width), sums[0].shape[1], first_column)
    here = pl.BlockSpec((rows, tile), lambda j: (0, first_column // tile + j))
    came = pl.BlockSpec((rows, tile), lambda j: (0, j))
    extra = [] if so_far is None else [so_far]
    return pl.pallas_call(
        functools.partial(finish_kernel, len(sums)),
        grid=(sums[0].shape[1] // tile,),
        in_specs=[here] + [came] * len(sums) + [pl.BlockSpec(memory_space=pl.ANY)] * len(extra),
        out_specs=here,
        out_shape=jax.ShapeDtypeStruct((rows, width), jnp.bfloat16),
        input_output_aliases={1 + len(sums): 0} if extra else {},
        compiler_params=params(),
        cost_estimate=cost(0, 5 * rows * sums[0].shape[1]),
    )(own, *sums, *extra)


def make_local(replicas, tensor):
    def local(
        attn_out,
        out_weight,
        store_factors,
        resident_factors,
        resident_ids,
        evict_slots,
        incoming,
        store_place,
        req_adapter,
    ):
        z = lax.axis_index("tensor")
        own = lax.axis_index("replica")
        width = out_weight.shape[1] // tensor
        tile = tile_of(width)
        slots = resident_factors.shape[0]
        store_rows = store_factors.shape[0]
        evict = evict_slots[0]
        even, odd = z % 2 == 0, z % 2 == 1
        not_first, not_last = z > 0, z < tensor - 1

        def edges(step, first):
            pairs = []
            for d in range(first, tensor - 1, 2):
                pairs += [(d, d + 1)] * (d <= step)
                pairs += [(d + 1, d)] * (d + 1 >= tensor - 1 - step)
            return pairs

        def swap(pairs):
            return pairs + [(b, a) for a, b in pairs if (b, a) not in pairs]

        def product(block, span, came_a, flag_a, came_b, flag_b, after):
            start, tiles = span
            first = jnp.clip(block, 0, tensor - 1) * (width // tile) + start
            if after is None:
                return first_term(attn_out, out_weight, z, tensor, tile, tiles)
            came = []
            for sums, flag in ((came_a, flag_a), (came_b, flag_b)):
                for (low, count), ref in sums:
                    if low < start + tiles and start < low + count:
                        came.append((ref, flag, low - start))
            out = term(attn_out, out_weight, first, tile, tiles, came, after)
            return out, out

        def step_of(step, came_x, came_y, after, between):
            right_block = tensor - 1 - step + z
            left_block = z + step + 1 - tensor
            pairs_x, pairs_y = edges(step, 0), edges(step, 1)
            xs, ys = [], []
            for span in spans(width, step, tensor - 1):
                if 2 * step < tensor - 1:
                    goes_right = 2 * z < tensor
                    block = jnp.where(goes_right, right_block, left_block)
                    flag_x = jnp.where(goes_right, odd, even & not_last)
                    flag_y = jnp.where(goes_right, even & not_first, odd & not_last)
                    for_x, last = product(block, span, came_x, flag_x, came_y, flag_y, after)
                    for_y = for_x
                else:
                    flag = jnp.where(even, not_first, not_last)
                    block = jnp.where(even, right_block, left_block)
                    for_x, last = product(block, span, [], flag, came_y, flag, after)
                    block = jnp.where(even, left_block, right_block)
                    for_y, last = product(block, span, came_x, flag, [], flag, last)
                pairs = pairs_x if step else swap(pairs_x)
                xs.append((span, lax.ppermute(for_x, "tensor", pairs)))
                if pairs_y:
                    ys.append((span, lax.ppermute(for_y, "tensor", pairs_y)))
                after = between(step, len(xs) - 1, last)
            return xs, ys, after

        matches = incoming[:, :, None] == jnp.arange(store_place.shape[0], dtype=jnp.int32)
        place = jnp.sum(jnp.where(matches, store_place, 0), axis=2)
        owners = place // store_rows
        spots = jnp.arange(place.shape[1], dtype=jnp.int32)
        earlier = jnp.sum(
            (owners[:, :, None] == owners[:, None, :]) & (spots[None, :] < spots[:, None]), axis=2
        ).astype(jnp.int32)
        asked = (owners == own)[:, :, None] & (
            earlier[:, :, None] == jnp.arange(CAP, dtype=jnp.int32)
        )
        rows_for = jnp.sum(jnp.where(asked, (place % store_rows)[:, :, None], 0), axis=1)
        hops = [exchange(replicas, hop) for hop in range(1, replicas)]
        send_rows = [
            lax.dynamic_index_in_dim(rows_for, to(own), 0, keepdims=False) for _, to in hops
        ]

        my_place = lax.dynamic_index_in_dim(place, own, 0, keepdims=False)
        my_earlier = lax.dynamic_index_in_dim(earlier, own, 0, keepdims=False)
        my_ids = lax.dynamic_index_in_dim(incoming, own, 0, keepdims=False)
        my_hop = hop_from(replicas, own, my_place // store_rows)
        my_index = jnp.where(my_hop == 0, my_place % store_rows, my_earlier)
        replaced = evict[None, :] == jnp.arange(slots, dtype=jnp.int32)[:, None]
        is_new = jnp.any(replaced, axis=1)

        def per_slot(new, old):
            chosen = jnp.sum(jnp.where(replaced, new[None, :], 0), axis=1)
            return jnp.where(is_new, chosen, old).astype(jnp.int32)

        kind = per_slot(1 + my_hop, jnp.zeros((slots,), jnp.int32))
        place_in = per_slot(my_index, jnp.arange(slots, dtype=jnp.int32))
        ids = per_slot(my_ids, resident_ids[0])
        index = jnp.concatenate(
            [jnp.where(kind == n, place_in, 0) for n in range(1 + replicas)]
        ).astype(jnp.int32)
        wanted = req_adapter[:, None]
        sources = [resident_factors, store_factors]
        if tensor == 4:
            inner = (z == 1) | (z == 2)
            rounds = [(edges(0, 0), True), ([(1, 2), (2, 1)], True), ([(1, 0), (2, 3)], inner)]
        else:
            bits = [1 << n for n in range(tensor.bit_length() - 1)]
            rounds = [(exchange(tensor, bit)[0], True) for bit in bits]
        state = {"mine": None, "theirs": None, "keep": None}

        def fetch(after):
            if not send_rows:
                return after
            picked = pick(store_factors, jnp.concatenate(send_rows).astype(jnp.int32), after)
            for piece, (pairs, _) in reversed(list(zip(picked, hops))):
                sources.insert(2, lax.ppermute(piece, "replica", pairs))
            return picked[0]

        def send_mine():
            state["theirs"] = None
            if rounds:
                pairs, state["keep"] = rounds.pop(0)
                state["theirs"] = lax.ppermute(state["mine"], "tensor", pairs)

        def shrink(after):
            state["mine"], state["expand"] = hold_slots(
                attn_out, wanted, ids, kind, index, sources, after
            )
            if tensor & (tensor - 1) == 0:
                send_mine()
            else:
                state["mine"] = lax.psum(state["mine"], "tensor")
            return state["mine"]

        def add_theirs(after):
            if state["theirs"] is None:
                return after
            state["mine"] = join(jnp.asarray(state["keep"]), state["mine"], state["theirs"], after)
            send_mine()
            return state["mine"]

        def between(step, piece, after):
            if step == 0 and piece == len(spans(width, 0, tensor - 1)) - 1:
                return fetch(after)
            if step == 1 and piece == 0:
                return shrink(after)
            return add_theirs(after)

        came_x, came_y, last = [], [], None
        for step in range(tensor - 1):
            came_x, came_y, last = step_of(step, came_x, came_y, last, between)
        if tensor < 3:
            last = shrink(last)
        while state["theirs"] is not None:
            last = add_theirs(last)
        total = own_term(
            attn_out,
            out_weight,
            z,
            state["mine"],
            wanted,
            ids,
            state["expand"].reshape(-1, width),
            last,
        )
        out = None
        for span in spans(width, tensor - 2, tensor - 1):
            sums = [ref for at, ref in came_x + came_y if at == span]
            out = finish(total, sums, span[0] * tile, out)
        return out

    return local


def solution(mesh):
    return jax.shard_map(
        make_local(mesh.shape["replica"], mesh.shape["tensor"]),
        mesh=mesh,
        in_specs=(
            P(("groups", "replica"), "tensor"),
            P("tensor", None),
            P(("groups", "replica"), None, None, "tensor"),
            P(("groups", "replica"), None, None, "tensor"),
            P(("groups", "replica"), None),
            P(("groups", "replica"), None),
            P("groups", None),
            P("groups"),
            P(("groups", "replica")),
        ),
        out_specs=P(("groups", "replica"), "tensor"),
        check_vma=False,
    )
```
